128 devices in a mesh: group: 8 (over y, core), sub: 16 (over z, x).
Axes of the slice: x: 4, y: 4, z: 4, core: 2. Of those that a mesh axis runs over, the one named last changes fastest.
Arguments:
- observations: float32 [64, 262144], P(None, ('group', 'sub')), may hold values from -6 to 6
- order: int32 [262144], P(('group', 'sub')), may hold values from 0 to 32767, as said below
- leaf_blocks: float32 [256, 1024, 1024], P(('group', 'sub')), as said below
- factors: float32 [8, 32, 262144], P(None, None, ('group', 'sub'))
Outputs:
- solution: float32 [64, 262144], P(None, ('group', 'sub'))
- residual: float32 [64, 262144], P(None, ('group', 'sub'))
The draws below stay inside these ranges and needn't reach their ends.
Inputs may be any that keep to these rules, and one draw needn't show every extreme that they name: `order`: within each aligned block of 32768 entries, every value 0 .. 32767 appears once. `leaf_blocks`: every block is symmetric positive definite.
All inputs are finite; a program needn't handle non-finite values.
Results may differ from the reference program's by a relative error of at most 0.0003.
Values sent between devices are 32-bit elements; how exact they have to be, the bound alone decides.
A program may use at most 128 MiB of HBM per device.

```python
import jax
import jax.numpy as jnp
from jax import lax

LEAF = 1024
RANK = 32
RHS = 64
ITERS = 4
POINTS = 262144
LEAVES = 256
GROUP_POINTS = 32768
LEVELS = 8


def draw_order(key, part):
    key = jax.random.fold_in(key, 1)
    keys = jax.random.split(key, POINTS // GROUP_POINTS)
    perms = jax.vmap(lambda single: jax.random.permutation(single, GROUP_POINTS))(keys)
    return perms.reshape(POINTS).astype(jnp.int32)


def draw_leaf_blocks(key, part):
    key = jax.random.fold_in(key, 2)
    first, second = jax.random.split(key)
    amplitude = 0.86 / LEAF ** 0.5
    noise = jax.random.uniform(first, (LEAVES, LEAF, LEAF), jnp.float32, -amplitude, amplitude)
    nugget = jnp.exp(jax.random.uniform(second, (LEAVES, LEAF), jnp.float32, jnp.log(0.1), 0.0))
    symmetric = 0.5 * (noise + jnp.swapaxes(noise, 1, 2))
    eye = jnp.eye(LEAF, dtype=jnp.float32)
    return (symmetric + eye[None] * (1.0 + nugget)[:, :, None]).astype(jnp.float32)


def draw_factors(key, part):
    key = jax.random.fold_in(key, 3)
    levels = jnp.arange(LEVELS, dtype=jnp.float32)
    scale = 0.5 ** 0.5 * (RANK * LEAF * 2.0 ** (levels + 1.0)) ** (-0.25)
    values = jnp.clip(jax.random.normal(key, (LEVELS, RANK, POINTS), jnp.float32), -4.0, 4.0)
    return (values * scale[:, None, None]).astype(jnp.float32)


def block_scale(own_key, extent, cuts, smallest, high):
    factor_of = 1.0
    for position, shards_of in cuts:
        steps = jax.random.uniform(jax.random.fold_in(jax.random.fold_in(own_key, 6), position), (shards_of,), jnp.float32, smallest / len(cuts), high / len(cuts))
        factor_of = factor_of * jnp.repeat(jnp.exp(steps), extent[position] // shards_of).reshape((-1,) + (1,) * (len(extent) - 1 - position))
    return factor_of


def scatter_about(stream_key, dims, scale, most, cuts=(), kind=jnp.bfloat16):
    gain = block_scale(stream_key, dims, cuts, -0.22, 0.18) if cuts else 1.0
    values = jax.random.normal(stream_key, dims, jnp.float32) * scale * gain
    return jnp.minimum(jnp.maximum(values, -most), most).astype(kind)


def setup_inputs(seed: int = 0) -> dict:
    streams_of = jax.random.split(jax.random.key(seed), 5)
    observations = scatter_about(streams_of[0], (RHS, POINTS), 1.0, 6.0, ((1, 128),), jnp.float32)
    order = draw_order(jax.random.fold_in(streams_of[4], 71), 0)
    leaf_blocks = draw_leaf_blocks(jax.random.fold_in(streams_of[4], 71), 0)
    factors = draw_factors(jax.random.fold_in(streams_of[4], 71), 0)
    return {"observations": observations, "order": order, "leaf_blocks": leaf_blocks, "factors": factors}


def apply_matrix(field, leaf_blocks, factors):
    rhs = field.shape[0]
    split = field.reshape(rhs, -1, LEAF)
    result = jnp.einsum('rbj,bjk->rbk', split, leaf_blocks, precision=lax.Precision.HIGHEST).reshape(rhs, -1)
    for level in range(LEVELS):
        width = LEAF * 2 ** (level + 1)
        pieces = field.reshape(rhs, -1, width)
        basis = factors[level].reshape(RANK, -1, width)
        coef = jnp.einsum('rns,kns->nrk', pieces, basis, precision=lax.Precision.HIGHEST)
        result = result + jnp.einsum('nrk,kns->rns', coef, basis, precision=lax.Precision.HIGHEST).reshape(rhs, -1)
    return result

def inner(left, right):
    return jnp.dot(left, right.T, precision=lax.Precision.HIGHEST)

def solve_spd(matrix, target):
    lower = jnp.linalg.cholesky(matrix)
    return jax.scipy.linalg.cho_solve((lower, True), target)

def reference(observations, order, leaf_blocks, factors):
    grouped = observations.reshape(RHS, -1, GROUP_POINTS)
    index = order.reshape(1, -1, GROUP_POINTS).astype(jnp.int32)
    right = jnp.take_along_axis(grouped, jnp.broadcast_to(index, grouped.shape), axis=2).reshape(RHS, -1)
    solution = jnp.zeros_like(right)
    residual = right
    direction = right
    norm_now = inner(residual, residual)
    for step in range(ITERS):
        image = apply_matrix(direction, leaf_blocks, factors)
        alpha = solve_spd(inner(direction, image), norm_now)
        solution = solution + jnp.dot(alpha.T, direction, precision=lax.Precision.HIGHEST)
        residual = residual - jnp.dot(alpha.T, image, precision=lax.Precision.HIGHEST)
        fresh = inner(residual, residual)
        beta = solve_spd(norm_now, fresh)
        direction = residual + jnp.dot(beta.T, direction, precision=lax.Precision.HIGHEST)
        norm_now = fresh
    return (solution, residual)
```

```python
import functools

import jax
import jax.numpy as jnp
from jax import lax
from jax.experimental import pallas as pl
from jax.experimental.pallas import tpu as pltpu
from jax.sharding import PartitionSpec as P

ITERS = 4
MESH = pl.DeviceIdType.MESH
F32 = jnp.float32
BF16 = jnp.bfloat16
EXACT = lax.Precision.HIGHEST
NT = (((1,), (1,)), ((), ()))


def halves(x):
    high = x.astype(BF16)
    return high, (x - high.astype(F32)).astype(BF16)


def dot3(left, right_high, right_low, dims=(((1,), (0,)), ((), ()))):
    rows = left.shape[0]
    high, low = halves(left)
    both = lax.dot_general(
        jnp.concatenate([high, low], 0), right_high, dims, preferred_element_type=F32
    )
    rest = lax.dot_general(high, right_low, dims, preferred_element_type=F32)
    return both[:rows] + (both[rows:] + rest)


def dot_exact(left, right, dims=(((1,), (0,)), ((), ()))):
    return lax.dot_general(left, right, dims, precision=EXACT, preferred_element_type=F32)


def eliminate(systems):
    size = systems[0].shape[0]
    rows = lax.broadcasted_iota(jnp.int32, systems[0].shape, 0)
    for k in range(size):
        done = []
        for system in systems:
            scaled = system[k : k + 1, :] * (1.0 / system[k : k + 1, k : k + 1])
            done.append(jnp.where(rows == k, scaled, system - system[:, k : k + 1] * scaled))
        systems = done
    return systems


def coefficient_stage(pieces, low_tile, high_tile, low_lanes, high_lanes, leaf_lanes):
    tiles = len(pieces[0])
    pairs = [[pieces[2 * h][t] + pieces[2 * h + 1][t] for t in range(tiles)] for h in range(2)]
    total = [pairs[0][t] + pairs[1][t] for t in range(tiles)]
    lane = lax.broadcasted_iota(jnp.int32, pieces[0][0].shape, 1)
    in_low = (lane >= low_lanes) & (lane < low_lanes + 32)
    in_high = (lane >= high_lanes) & (lane < high_lanes + 32)
    parts = [
        jnp.where(in_low, pairs[0][low_tile], jnp.where(in_high, total[high_tile], 0.0)),
        jnp.where(in_low, pairs[1][low_tile], 0.0),
    ]
    if leaf_lanes:
        parts = parts + [jnp.zeros_like(parts[0])] * 2
        parts = [jnp.where(lane < 32, pieces[m][0], parts[m]) for m in range(4)]
    return pairs, total, parts


def node_products(parts):
    side = jnp.concatenate(parts, 1)
    return dot_exact(side, jnp.concatenate([jnp.zeros_like(side), side], 0), NT)


def kernel(
    obs_ref, order_ref, leaf_ref, factors_ref,
    solution_ref, residual_ref,
    stage, leaf_high, leaf_low, basis_high, basis_low, across_high, across_low,
    gathered, table, picked, order_in, order_smem, ready,
    r_ref, w_ref, d_ref, s_ref, x_ref, own_ref,
    x_coef, x_sum, z_coef, z_sum, c_coef, c_sum, y_coef, y_sum,
    load_sem, smem_sem, order_send, order_recv, obs_send, obs_recv, back_send, back_recv,
    ring_send, ring_recv,
):
    group, sub = lax.axis_index("group"), lax.axis_index("sub")
    x = lax.rem(sub, 4)
    z = lax.div(sub, 4)
    core = lax.rem(group, 2)
    y = lax.div(group, 2)
    rhs, points = obs_ref.shape
    width = rhs // 4

    loads = [
        pltpu.make_async_copy(leaf_ref.at[b], stage.at[b], load_sem.at[b]) for b in range(2)
    ]
    for load in loads:
        load.start()

    def on_x(k):
        return (group, z * 4 + (x ^ k))

    def on_z(k):
        return (group, (z ^ k) * 4 + x)

    def on_core(k):
        return (y * 2 + (core ^ k), sub)

    def on_y(k):
        return ((y ^ k) * 2 + core, sub)

    barrier = pltpu.get_barrier_semaphore()
    for k in range(1, 16):
        pl.semaphore_signal(barrier, inc=1, device_id=(group, sub ^ k), device_id_type=MESH)
    for k in range(1, 4):
        pl.semaphore_signal(barrier, inc=1, device_id=on_y(k), device_id_type=MESH)
    pl.semaphore_signal(barrier, inc=1, device_id=on_core(1), device_id_type=MESH)
    pl.semaphore_wait(barrier, 19)

    order_copies = []
    for k in range(1, 4):
        copy = pltpu.make_async_remote_copy(
            src_ref=order_ref, dst_ref=order_in.at[k],
            send_sem=order_send.at[k], recv_sem=order_recv.at[k],
            device_id=on_x(k), device_id_type=MESH,
        )
        copy.start()
        order_copies.append(copy)
    obs_copies = {}
    for k in (1, 4, 2, 3, 5, 7, 8, 12, 13, 6, 9, 10, 11, 14, 15):
        quarter = x ^ (k % 4)
        copy = pltpu.make_async_remote_copy(
            src_ref=obs_ref.at[pl.ds(pl.multiple_of(quarter * width, width), width), :],
            dst_ref=gathered.at[k],
            send_sem=obs_send.at[k], recv_sem=obs_recv.at[k],
            device_id=(group, sub ^ k), device_id_type=MESH,
        )
        copy.start()
        obs_copies[k] = copy

    for b in range(2):
        loads[b].wait()

        def cut(i, _, b=b):
            rows = pl.ds(pl.multiple_of(i * 64, 64), 64)
            leaf_high[b, rows, :], leaf_low[b, rows, :] = halves(stage[b, rows, :])
            return 0

        lax.fori_loop(0, leaf_ref.shape[1] // 64, cut, 0)

    def turn(i, _):
        cols = pl.ds(pl.multiple_of(i * 128, 128), 128)
        part = factors_ref[:, cols]
        basis_high[:, cols], basis_low[:, cols] = halves(part)
        across_high[cols, :], across_low[cols, :] = halves(part.T)
        return 0

    lax.fori_loop(0, points // 128, turn, 0)

    own_order = pltpu.make_async_copy(order_ref, order_smem.at[0], smem_sem.at[0])
    own_order.start()
    for k in range(1, 4):
        order_copies[k - 1].wait()
        copy = pltpu.make_async_copy(order_in.at[k], order_smem.at[k], smem_sem.at[k])
        copy.start()
        copy.wait()
    own_order.wait()

    def tabulate(block, k):
        def step(i, _):
            cols = pl.ds(pl.multiple_of(i * 128, 128), 128)
            rows = pl.ds(pl.multiple_of((sub ^ k) * points + i * 128, 128), 128)
            table[rows, :] = block(cols).T
            return 0

        lax.fori_loop(0, points // 128, step, 0)

    mine = pl.ds(pl.multiple_of(x * width, width), width)
    tabulate(lambda cols: obs_ref[mine, cols], 0)
    for k in (1, 4, 2, 3, 5, 7, 8, 12, 13, 6, 9, 10, 11, 14, 15):
        obs_copies[k].wait()
        tabulate(lambda cols, k=k: gathered[k, :, cols], k)

    back_copies = []
    for k in (2, 1, 3, 0):

        def pick(i, _, k=k):
            for j in range(128):
                picked[pl.ds(i * 128 + j, 1), :] = table[pl.ds(order_smem[k, i, j], 1), :]
            return 0

        lax.fori_loop(0, points // 128, pick, 0)

        def lay(i, _, k=k):
            cols = pl.ds(pl.multiple_of(i * 128, 128), 128)
            turned = picked[pl.ds(pl.multiple_of(i * 128, 128), 128), :].T
            if k:
                ready[k, :, cols] = turned
            else:
                r_ref[mine, cols] = turned
            return 0

        lax.fori_loop(0, points // 128, lay, 0)
        if k:
            copy = pltpu.make_async_remote_copy(
                src_ref=ready.at[k], dst_ref=r_ref.at[mine, :],
                send_sem=back_send.at[k], recv_sem=back_recv.at[k],
                device_id=on_x(k), device_id_type=MESH,
            )
            copy.start()
            back_copies.append(copy)
    for copy in back_copies:
        copy.wait()

    def send(kind, turn_at, buffer, slot, peer, count):
        copies = []
        for k in range(1, count):
            copy = pltpu.make_async_remote_copy(
                src_ref=buffer.at[turn_at, slot], dst_ref=buffer.at[turn_at, slot],
                send_sem=ring_send.at[kind, k], recv_sem=ring_recv.at[kind, turn_at, k],
                device_id=peer(k), device_id_type=MESH,
            )
            copy.start()
            copies.append(copy)
        return copies

    def finish(copies):
        for copy in copies:
            copy.wait()

    d_ref[...] = jnp.zeros_like(d_ref)
    s_ref[...] = jnp.zeros_like(s_ref)
    x_ref[...] = jnp.zeros_like(x_ref)
    half = points // 2
    lane = lax.broadcasted_iota(jnp.int32, (rhs, 128), 1)
    eye = (lax.broadcasted_iota(jnp.int32, (rhs, rhs), 0) == lax.broadcasted_iota(jnp.int32, (rhs, rhs), 1)).astype(F32)

    def iteration(step, carry):
        inverse, curv_before = carry
        at = lax.rem(step, 2)
        r = r_ref[...]
        own = dot3(r, across_high[...], across_low[...])
        x_coef[at, x] = own
        coef_copies = send(0, at, x_coef, x, on_x, 4)

        for b in range(2):
            cols = slice(b * half, (b + 1) * half)
            w_ref[:, cols] = dot3(r_ref[:, cols], leaf_high[b], leaf_low[b])
        rw_high, rw_low = halves(jnp.concatenate([r_ref[...], w_ref[...]], 0))
        x_sum[at, x] = dot3(r_ref[...], rw_high, rw_low, NT)
        sum_copies = send(1, at, x_sum, x, on_x, 4)

        finish(coef_copies)
        pieces = [[x_coef[at, m, :, 0:128], x_coef[at, m, :, 128:256]] for m in range(4)]
        pairs, total, parts = coefficient_stage(pieces, 0, 0, 32, 64, True)
        z_coef[at, z, :, 0:128] = total[0]
        z_coef[at, z, :, 128:256] = total[1]
        coef_copies = send(2, at, z_coef, z, on_z, 4)
        first = jnp.where(lane < 32, own[:, 0:128], jnp.where(x < 2, pairs[0][0], pairs[1][0]))
        first = jnp.where(lane < 64, first, total[0])
        extra = node_products(parts)
        finish(sum_copies)
        z_sum[at, z] = ((x_sum[at, 0] + x_sum[at, 1]) + (x_sum[at, 2] + x_sum[at, 3])) + extra
        sum_copies = send(3, at, z_sum, z, on_z, 4)

        finish(coef_copies)
        pieces = [[z_coef[at, m, :, 0:128], z_coef[at, m, :, 128:256]] for m in range(4)]
        pairs, total, parts = coefficient_stage(pieces, 0, 1, 96, 0, False)
        c_coef[at, core] = total[1]
        coef_copies = send(4, at, c_coef, core, on_core, 2)
        first = jnp.where(lane < 96, first, jnp.where(z < 2, pairs[0][0], pairs[1][0]))
        second = total[1]
        extra = node_products(parts)
        finish(sum_copies)
        c_sum[at, core] = ((z_sum[at, 0] + z_sum[at, 1]) + (z_sum[at, 2] + z_sum[at, 3])) + extra
        sum_copies = send(5, at, c_sum, core, on_core, 2)

        finish(coef_copies)
        chip = c_coef[at, 0] + c_coef[at, 1]
        y_coef[at, y] = chip
        coef_copies = send(6, at, y_coef, y, on_y, 4)
        second = jnp.where(lane < 32, second, chip)
        extra = node_products([jnp.where((lane >= 32) & (lane < 64), chip, 0.0)])
        finish(sum_copies)
        y_sum[at, y] = (c_sum[at, 0] + c_sum[at, 1]) + extra
        sum_copies = send(7, at, y_sum, y, on_y, 4)

        finish(coef_copies)
        pieces = [[y_coef[at, m]] for m in range(4)]
        pairs, total, parts = coefficient_stage(pieces, 0, 0, 64, 96, False)
        second = jnp.where(lane < 64, second, jnp.where(y < 2, pairs[0][0], pairs[1][0]))
        second = jnp.where(lane < 96, second, total[0])
        extra = node_products(parts)
        own_ref[:, 0:128] = first
        own_ref[:, 128:256] = second
        coefs = own_ref[...]
        for c in range(4):
            cols = slice(c * 512, (c + 1) * 512)
            w_ref[:, cols] = w_ref[:, cols] + dot3(coefs, basis_high[:, cols], basis_low[:, cols])
        finish(sum_copies)
        both = ((y_sum[at, 0] + y_sum[at, 1]) + (y_sum[at, 2] + y_sum[at, 3])) + extra

        norm, along = both[:, :rhs], both[:, rhs:]
        beta = dot_exact(inverse, norm)
        curv = along - dot_exact(beta.T, dot_exact(curv_before, beta))

        def weights(matrix):
            high, low = halves(matrix)
            high, low = high.astype(F32), low.astype(F32)
            return jnp.concatenate([high, high, low, low], 0).T.astype(BF16)

        def times(weight, array):
            high, low = halves(array)
            return jnp.dot(
                weight, jnp.concatenate([high, low, high, low], 0), preferred_element_type=F32
            )

        beta_weight = weights(beta)
        def advance(c, _):
            cols = pl.ds(pl.multiple_of(c * 512, 512), 512)
            d_ref[:, cols] = r_ref[:, cols] + times(beta_weight, d_ref[:, cols])
            s_ref[:, cols] = w_ref[:, cols] + times(beta_weight, s_ref[:, cols])
            return 0

        lax.fori_loop(0, 4, advance, 0)
        solved, inverted = eliminate(
            [jnp.concatenate([curv, norm], 1), jnp.concatenate([norm, eye], 1)]
        )
        alpha_weight = weights(solved[:, rhs:])

        def improve(c, _):
            cols = pl.ds(pl.multiple_of(c * 512, 512), 512)
            r_ref[:, cols] = r_ref[:, cols] - times(alpha_weight, s_ref[:, cols])
            x_ref[:, cols] = x_ref[:, cols] + times(alpha_weight, d_ref[:, cols])
            return 0

        lax.fori_loop(0, 4, improve, 0)
        return inverted[:, rhs:], curv

    zeros = jnp.zeros((rhs, rhs), F32)
    lax.fori_loop(0, ITERS, iteration, (zeros, zeros))
    solution_ref[...] = x_ref[...]
    residual_ref[...] = r_ref[...]


def shards(observations, order, leaf_blocks, factors):
    rhs, points = observations.shape
    leaves, leaf = leaf_blocks.shape[:2]
    rank = factors.shape[0] * factors.shape[1]
    width = rhs // 4
    vector = pltpu.VMEM((rhs, points), F32)
    dma = pltpu.SemaphoreType.DMA
    vmem = pl.BlockSpec(memory_space=pltpu.VMEM)
    out = jax.ShapeDtypeStruct((rhs, points), F32)
    return pl.pallas_call(
        kernel,
        out_shape=(out, out),
        in_specs=[vmem, vmem, pl.BlockSpec(memory_space=pl.ANY), vmem],
        out_specs=(vmem, vmem),
        scratch_shapes=[
            pltpu.VMEM((leaves, leaf, leaf), F32),
            pltpu.VMEM((leaves, leaf, leaf), BF16),
            pltpu.VMEM((leaves, leaf, leaf), BF16),
            pltpu.VMEM((rank, points), BF16),
            pltpu.VMEM((rank, points), BF16),
            pltpu.VMEM((points, rank), BF16),
            pltpu.VMEM((points, rank), BF16),
            pltpu.VMEM((16, width, points), F32),
            pltpu.VMEM((16 * points, width), F32),
            pltpu.VMEM((points, width), F32),
            pltpu.VMEM((4, points // 128, 128), jnp.int32),
            pltpu.SMEM((4, points // 128, 128), jnp.int32),
            pltpu.VMEM((4, width, points), F32),
            vector, vector, vector, vector, vector,
            pltpu.VMEM((rhs, rank), F32),
            pltpu.VMEM((2, 4, rhs, rank), F32),
            pltpu.VMEM((2, 4, rhs, 2 * rhs), F32),
            pltpu.VMEM((2, 4, rhs, rank), F32),
            pltpu.VMEM((2, 4, rhs, 2 * rhs), F32),
            pltpu.VMEM((2, 2, rhs, rank // 2), F32),
            pltpu.VMEM((2, 2, rhs, 2 * rhs), F32),
            pltpu.VMEM((2, 4, rhs, rank // 2), F32),
            pltpu.VMEM((2, 4, rhs, 2 * rhs), F32),
            dma((2,)), dma((4,)), dma((4,)), dma((4,)),
            dma((16,)), dma((16,)), dma((4,)), dma((4,)),
            dma((8, 4)), dma((8, 2, 4)),
        ],
        compiler_params=pltpu.CompilerParams(
            collective_id=0, has_side_effects=True, vmem_limit_bytes=60 * 2**20
        ),
        name="block_cg",
    )(observations, order.reshape(points // 128, 128), leaf_blocks, factors.reshape(rank, points))


def solution(mesh):
    in_specs = (
        P(None, ("group", "sub")),
        P(("group", "sub")),
        P(("group", "sub"), None, None),
        P(None, None, ("group", "sub")),
    )
    out_specs = (P(None, ("group", "sub")), P(None, ("group", "sub")))
    return jax.shard_map(shards, mesh=mesh, in_specs=in_specs, out_specs=out_specs, check_vma=False)
```

```python
import functools

import jax
import jax.numpy as jnp
from jax import lax
from jax.experimental import pallas as pl
from jax.experimental.pallas import tpu as pltpu
from jax.sharding import PartitionSpec as P

ITERS = 4
MESH = pl.DeviceIdType.MESH
F32 = jnp.float32
BF16 = jnp.bfloat16
EXACT = lax.Precision.HIGHEST
NT = (((1,), (1,)), ((), ()))


def halves(x):
    high = x.astype(BF16)
    return high, (x - high.astype(F32)).astype(BF16)


def dot3(left, right_high, right_low, dims=(((1,), (0,)), ((), ()))):
    rows = left.shape[0]
    high, low = halves(left)
    both = lax.dot_general(
        jnp.concatenate([high, low], 0), right_high, dims, preferred_element_type=F32
    )
    rest = lax.dot_general(high, right_low, dims, preferred_element_type=F32)
    return both[:rows] + (both[rows:] + rest)


def dot_exact(left, right, dims=(((1,), (0,)), ((), ()))):
    return lax.dot_general(left, right, dims, precision=EXACT, preferred_element_type=F32)


def eliminate(systems):
    size = systems[0].shape[0]
    rows = lax.broadcasted_iota(jnp.int32, systems[0].shape, 0)
    for k in range(size):
        done = []
        for system in systems:
            scaled = system[k : k + 1, :] * (1.0 / system[k : k + 1, k : k + 1])
            done.append(jnp.where(rows == k, scaled, system - system[:, k : k + 1] * scaled))
        systems = done
    return systems


def coefficient_stage(pieces, low_tile, high_tile, low_lanes, high_lanes, leaf_lanes):
    tiles = len(pieces[0])
    pairs = [[pieces[2 * h][t] + pieces[2 * h + 1][t] for t in range(tiles)] for h in range(2)]
    total = [pairs[0][t] + pairs[1][t] for t in range(tiles)]
    lane = lax.broadcasted_iota(jnp.int32, pieces[0][0].shape, 1)
    in_low = (lane >= low_lanes) & (lane < low_lanes + 32)
    in_high = (lane >= high_lanes) & (lane < high_lanes + 32)
    parts = [
        jnp.where(in_low, pairs[0][low_tile], jnp.where(in_high, total[high_tile], 0.0)),
        jnp.where(in_low, pairs[1][low_tile], 0.0),
    ]
    if leaf_lanes:
        parts = parts + [jnp.zeros_like(parts[0])] * 2
        parts = [jnp.where(lane < 32, pieces[m][0], parts[m]) for m in range(4)]
    return pairs, total, parts


def node_products(parts):
    side = jnp.concatenate(parts, 1)
    return dot_exact(side, jnp.concatenate([jnp.zeros_like(side), side], 0), NT)


def kernel(
    obs_ref, order_ref, leaf_ref, factors_ref,
    solution_ref, residual_ref,
    stage, leaf_high, leaf_low, basis_high, basis_low, across_high, across_low,
    gathered, table, picked, order_in, source_in, order_smem, ready,
    r_ref, w_ref, d_ref, s_ref, x_ref, own_ref,
    x_coef, x_sum, z_coef, z_sum, c_coef, c_sum, y_coef, y_sum,
    load_sem, smem_sem, order_send, order_recv, near_send, near_recv, far_send, far_recv, back_send, back_recv,
    ring_send, ring_recv,
):
    group, sub = lax.axis_index("group"), lax.axis_index("sub")
    x = lax.rem(sub, 4)
    z = lax.div(sub, 4)
    core = lax.rem(group, 2)
    y = lax.div(group, 2)
    rhs, points = obs_ref.shape

    loads = [
        pltpu.make_async_copy(leaf_ref.at[b], stage.at[b], load_sem.at[b]) for b in range(2)
    ]
    for load in loads:
        load.start()

    def on_x(k):
        return (group, z * 4 + (x ^ k))

    def on_z(k):
        return (group, (z ^ k) * 4 + x)

    def on_core(k):
        return (y * 2 + (core ^ k), sub)

    def on_y(k):
        return ((y ^ k) * 2 + core, sub)

    def on_diagonal(j):
        return (group, lax.rem(z + j, 4) * 4 + lax.rem(x + j, 4))

    barrier = pltpu.get_barrier_semaphore()
    for k in range(1, 4):
        for peer in (on_x(k), on_z(k), on_y(k), on_diagonal(k)):
            pl.semaphore_signal(barrier, inc=1, device_id=peer, device_id_type=MESH)
    pl.semaphore_signal(barrier, inc=1, device_id=on_core(1), device_id_type=MESH)
    pl.semaphore_wait(barrier, 13)

    def remote(source, target, sent, received, peer):
        copy = pltpu.make_async_remote_copy(
            src_ref=source, dst_ref=target, send_sem=sent, recv_sem=received,
            device_id=peer, device_id_type=MESH,
        )
        copy.start()
        return copy

    width = rhs // 8
    by_x, by_z = slice(0, width), slice(width, 2 * width)

    def x_rows(at):
        return pl.ds(pl.multiple_of(at * width, width), width)

    def z_rows(at):
        return pl.ds(pl.multiple_of(rhs // 2 + at * width, width), width)

    order_copies = [
        remote(order_ref, order_in.at[4 - j], order_send.at[j], order_recv.at[4 - j], on_diagonal(j))
        for j in range(1, 4)
    ]
    near = []
    for k in range(1, 4):
        near.append((
            remote(obs_ref.at[x_rows(x ^ k), :], gathered.at[sub, by_x], near_send.at[0, k], near_recv.at[0, k], on_x(k)),
            remote(obs_ref.at[z_rows(z ^ k), :], gathered.at[sub, by_z], near_send.at[1, k], near_recv.at[1, k], on_z(k)),
        ))
    far = []
    for m in range(1, 4):
        far.append(remote(obs_ref.at[x_rows(x), :], gathered.at[sub, by_x], far_send.at[0, 0, m], far_recv.at[0, 0, m], on_z(m)))
        far.append(remote(obs_ref.at[z_rows(z), :], gathered.at[sub, by_z], far_send.at[1, 0, m], far_recv.at[1, 0, m], on_x(m)))
    gathered[sub, by_x, :] = obs_ref[x_rows(x), :]
    gathered[sub, by_z, :] = obs_ref[z_rows(z), :]

    def cut_leaf(b):
        loads[b].wait()

        def cut(i, _):
            rows = pl.ds(pl.multiple_of(i * 64, 64), 64)
            leaf_high[b, rows, :], leaf_low[b, rows, :] = halves(stage[b, rows, :])
            return 0

        lax.fori_loop(0, leaf_ref.shape[1] // 64, cut, 0)

    cut_leaf(0)
    for k in range(1, 4):
        from_x, from_z = near[k - 1]
        from_x.wait()
        slot = gathered.at[z * 4 + (x ^ k), by_x]
        for m in range(1, 4):
            far.append(remote(slot, slot, far_send.at[0, k, m], far_recv.at[0, k, m], on_z(m)))
        from_z.wait()
        slot = gathered.at[(z ^ k) * 4 + x, by_z]
        for m in range(1, 4):
            far.append(remote(slot, slot, far_send.at[1, k, m], far_recv.at[1, k, m], on_x(m)))

    order_in[0] = order_ref[...]
    for copy in order_copies:
        copy.wait()
    for j in range(4):
        position = order_in[j]
        source_in[j] = lax.rem(lax.div(position, points), 8)
        order_in[j] = lax.div(position, points * 8) * points + lax.rem(position, points)
    to_scalar = pltpu.make_async_copy(order_in, order_smem, smem_sem)
    to_scalar.start()
    cut_leaf(1)

    def turn(i, _):
        cols = pl.ds(pl.multiple_of(i * 128, 128), 128)
        part = factors_ref[:, cols]
        basis_high[:, cols], basis_low[:, cols] = halves(part)
        across_high[cols, :], across_low[cols, :] = halves(part.T)
        return 0

    lax.fori_loop(0, points // 128, turn, 0)
    to_scalar.wait()
    for copy in far:
        copy.wait()

    def tabulate(i, _):
        for j in range(4):
            cols = pl.ds(pl.multiple_of(i * 512 + j * 128, 128), 128)
            for h in range(2):
                rows = pl.ds(pl.multiple_of(h * points + i * 512 + j * 128, 128), 128)
                table[rows, :] = gathered[8 * h : 8 * h + 8, :, cols].reshape(128, 128).T
        return 0

    lax.fori_loop(0, points // 512, tabulate, 0)

    back_copies = []
    for j in (2, 1, 3, 0):

        def pick(i, _, j=j):
            for n in range(128):
                picked[pl.ds(i * 128 + n, 1), :] = table[pl.ds(order_smem[j, i, n], 1), :]
            return 0

        lax.fori_loop(0, points // 128, pick, 0)

        def lay(i, _, j=j):
            for n in range(4):
                cols = pl.ds(pl.multiple_of(i * 512 + n * 128, 128), 128)
                turned = picked[cols, :].T
                source = source_in[j, pl.ds(i * 4 + n, 1), :]
                chosen = jnp.where(source == 0, turned[0 : 2 * width], 0.0)
                for g in range(1, 8):
                    chosen = jnp.where(source == g, turned[2 * width * g : 2 * width * (g + 1)], chosen)
                if j:
                    ready[j, :, cols] = chosen
                else:
                    r_ref[x_rows(x), cols] = chosen[by_x]
                    r_ref[z_rows(z), cols] = chosen[by_z]
            return 0

        lax.fori_loop(0, points // 512, lay, 0)
        if j:
            peer = on_diagonal(j)
            back_copies.append(remote(ready.at[j, by_x], r_ref.at[x_rows(x), :], back_send.at[0, j], back_recv.at[0, j], peer))
            back_copies.append(remote(ready.at[j, by_z], r_ref.at[z_rows(z), :], back_send.at[1, j], back_recv.at[1, j], peer))
    for copy in back_copies:
        copy.wait()

    def send(kind, turn_at, buffer, slot, peer, count):
        copies = []
        for k in range(1, count):
            copy = pltpu.make_async_remote_copy(
                src_ref=buffer.at[turn_at, slot], dst_ref=buffer.at[turn_at, slot],
                send_sem=ring_send.at[kind, k], recv_sem=ring_recv.at[kind, turn_at, k],
                device_id=peer(k), device_id_type=MESH,
            )
            copy.start()
            copies.append(copy)
        return copies

    def finish(copies):
        for copy in copies:
            copy.wait()

    d_ref[...] = jnp.zeros_like(d_ref)
    s_ref[...] = jnp.zeros_like(s_ref)
    x_ref[...] = jnp.zeros_like(x_ref)
    half = points // 2
    lane = lax.broadcasted_iota(jnp.int32, (rhs, 128), 1)
    eye = (lax.broadcasted_iota(jnp.int32, (rhs, rhs), 0) == lax.broadcasted_iota(jnp.int32, (rhs, rhs), 1)).astype(F32)

    def iteration(step, carry):
        inverse, curv_before = carry
        at = lax.rem(step, 2)
        r = r_ref[...]
        own = dot3(r, across_high[...], across_low[...])
        x_coef[at, x] = own
        coef_copies = send(0, at, x_coef, x, on_x, 4)

        for b in range(2):
            cols = slice(b * half, (b + 1) * half)
            w_ref[:, cols] = dot3(r_ref[:, cols], leaf_high[b], leaf_low[b])
        rw_high, rw_low = halves(jnp.concatenate([r_ref[...], w_ref[...]], 0))
        x_sum[at, x] = dot3(r_ref[...], rw_high, rw_low, NT)
        sum_copies = send(1, at, x_sum, x, on_x, 4)

        finish(coef_copies)
        pieces = [[x_coef[at, m, :, 0:128], x_coef[at, m, :, 128:256]] for m in range(4)]
        pairs, total, parts = coefficient_stage(pieces, 0, 0, 32, 64, True)
        z_coef[at, z, :, 0:128] = total[0]
        z_coef[at, z, :, 128:256] = total[1]
        coef_copies = send(2, at, z_coef, z, on_z, 4)
        first = jnp.where(lane < 32, own[:, 0:128], jnp.where(x < 2, pairs[0][0], pairs[1][0]))
        first = jnp.where(lane < 64, first, total[0])
        extra = node_products(parts)
        finish(sum_copies)
        z_sum[at, z] = ((x_sum[at, 0] + x_sum[at, 1]) + (x_sum[at, 2] + x_sum[at, 3])) + extra
        sum_copies = send(3, at, z_sum, z, on_z, 4)

        finish(coef_copies)
        pieces = [[z_coef[at, m, :, 0:128], z_coef[at, m, :, 128:256]] for m in range(4)]
        pairs, total, parts = coefficient_stage(pieces, 0, 1, 96, 0, False)
        c_coef[at, core] = total[1]
        coef_copies = send(4, at, c_coef, core, on_core, 2)
        first = jnp.where(lane < 96, first, jnp.where(z < 2, pairs[0][0], pairs[1][0]))
        second = total[1]
        extra = node_products(parts)
        finish(sum_copies)
        c_sum[at, core] = ((z_sum[at, 0] + z_sum[at, 1]) + (z_sum[at, 2] + z_sum[at, 3])) + extra
        sum_copies = send(5, at, c_sum, core, on_core, 2)

        finish(coef_copies)
        chip = c_coef[at, 0] + c_coef[at, 1]
        y_coef[at, y] = chip
        coef_copies = send(6, at, y_coef, y, on_y, 4)
        second = jnp.where(lane < 32, second, chip)
        extra = node_products([jnp.where((lane >= 32) & (lane < 64), chip, 0.0)])
        finish(sum_copies)
        y_sum[at, y] = (c_sum[at, 0] + c_sum[at, 1]) + extra
        sum_copies = send(7, at, y_sum, y, on_y, 4)

        finish(coef_copies)
        pieces = [[y_coef[at, m]] for m in range(4)]
        pairs, total, parts = coefficient_stage(pieces, 0, 0, 64, 96, False)
        second = jnp.where(lane < 64, second, jnp.where(y < 2, pairs[0][0], pairs[1][0]))
        second = jnp.where(lane < 96, second, total[0])
        extra = node_products(parts)
        own_ref[:, 0:128] = first
        own_ref[:, 128:256] = second
        coefs = own_ref[...]
        for c in range(4):
            cols = slice(c * 512, (c + 1) * 512)
            w_ref[:, cols] = w_ref[:, cols] + dot3(coefs, basis_high[:, cols], basis_low[:, cols])
        finish(sum_copies)
        both = ((y_sum[at, 0] + y_sum[at, 1]) + (y_sum[at, 2] + y_sum[at, 3])) + extra

        norm, along = both[:, :rhs], both[:, rhs:]
        beta = dot_exact(inverse, norm)
        curv = along - dot_exact(beta.T, dot_exact(curv_before, beta))

        def weights(matrix):
            high, low = halves(matrix)
            high, low = high.astype(F32), low.astype(F32)
            return jnp.concatenate([high, high, low, low], 0).T.astype(BF16)

        def times(weight, array):
            high, low = halves(array)
            return jnp.dot(
                weight, jnp.concatenate([high, low, high, low], 0), preferred_element_type=F32
            )

        beta_weight = weights(beta)
        def advance(c, _):
            cols = pl.ds(pl.multiple_of(c * 512, 512), 512)
            d_ref[:, cols] = r_ref[:, cols] + times(beta_weight, d_ref[:, cols])
            s_ref[:, cols] = w_ref[:, cols] + times(beta_weight, s_ref[:, cols])
            return 0

        lax.fori_loop(0, 4, advance, 0)
        solved, inverted = eliminate(
            [jnp.concatenate([curv, norm], 1), jnp.concatenate([norm, eye], 1)]
        )
        alpha_weight = weights(solved[:, rhs:])

        def improve(c, _):
            cols = pl.ds(pl.multiple_of(c * 512, 512), 512)
            r_ref[:, cols] = r_ref[:, cols] - times(alpha_weight, s_ref[:, cols])
            x_ref[:, cols] = x_ref[:, cols] + times(alpha_weight, d_ref[:, cols])
            return 0

        lax.fori_loop(0, 4, improve, 0)
        return inverted[:, rhs:], curv

    zeros = jnp.zeros((rhs, rhs), F32)
    lax.fori_loop(0, ITERS, iteration, (zeros, zeros))
    solution_ref[...] = x_ref[...]
    residual_ref[...] = r_ref[...]


def shards(observations, order, leaf_blocks, factors):
    rhs, points = observations.shape
    leaves, leaf = leaf_blocks.shape[:2]
    rank = factors.shape[0] * factors.shape[1]
    vector = pltpu.VMEM((rhs, points), F32)
    dma = pltpu.SemaphoreType.DMA
    vmem = pl.BlockSpec(memory_space=pltpu.VMEM)
    out = jax.ShapeDtypeStruct((rhs, points), F32)
    return pl.pallas_call(
        kernel,
        out_shape=(out, out),
        in_specs=[vmem, vmem, pl.BlockSpec(memory_space=pl.ANY), vmem],
        out_specs=(vmem, vmem),
        scratch_shapes=[
            pltpu.VMEM((leaves, leaf, leaf), F32),
            pltpu.VMEM((leaves, leaf, leaf), BF16),
            pltpu.VMEM((leaves, leaf, leaf), BF16),
            pltpu.VMEM((rank, points), BF16),
            pltpu.VMEM((rank, points), BF16),
            pltpu.VMEM((points, rank), BF16),
            pltpu.VMEM((points, rank), BF16),
            pltpu.VMEM((16, rhs // 4, points), F32),
            pltpu.VMEM((2 * points, 128), F32),
            pltpu.VMEM((points, 128), F32),
            pltpu.VMEM((4, points // 128, 128), jnp.int32),
            pltpu.VMEM((4, points // 128, 128), jnp.int32),
            pltpu.SMEM((4, points // 128, 128), jnp.int32),
            pltpu.VMEM((4, rhs // 4, points), F32),
            vector, vector, vector, vector, vector,
            pltpu.VMEM((rhs, rank), F32),
            pltpu.VMEM((2, 4, rhs, rank), F32),
            pltpu.VMEM((2, 4, rhs, 2 * rhs), F32),
            pltpu.VMEM((2, 4, rhs, rank), F32),
            pltpu.VMEM((2, 4, rhs, 2 * rhs), F32),
            pltpu.VMEM((2, 2, rhs, rank // 2), F32),
            pltpu.VMEM((2, 2, rhs, 2 * rhs), F32),
            pltpu.VMEM((2, 4, rhs, rank // 2), F32),
            pltpu.VMEM((2, 4, rhs, 2 * rhs), F32),
            dma((2,)), dma, dma((4,)), dma((4,)),
            dma((2, 4)), dma((2, 4)), dma((2, 4, 4)), dma((2, 4, 4)), dma((2, 4)), dma((2, 4)),
            dma((8, 4)), dma((8, 2, 4)),
        ],
        compiler_params=pltpu.CompilerParams(
            collective_id=0, has_side_effects=True, vmem_limit_bytes=60 * 2**20
        ),
        name="block_cg",
    )(observations, order.reshape(points // 128, 128), leaf_blocks, factors.reshape(rank, points))


def solution(mesh):
    in_specs = (
        P(None, ("group", "sub")),
        P(("group", "sub")),
        P(("group", "sub"), None, None),
        P(None, None, ("group", "sub")),
    )
    out_specs = (P(None, ("group", "sub")), P(None, ("group", "sub")))
    return jax.shard_map(shards, mesh=mesh, in_specs=in_specs, out_specs=out_specs, check_vma=False)
```

```python
import functools

import jax
import jax.numpy as jnp
from jax import lax
from jax.experimental import pallas as pl
from jax.experimental.pallas import tpu as pltpu
from jax.sharding import PartitionSpec as P

ITERS = 4
FAR_FIRST = (10, 2, 8, 6, 14, 9, 11, 3, 7, 13, 15, 12, 5, 1, 4)
MESH = pl.DeviceIdType.MESH
F32 = jnp.float32
BF16 = jnp.bfloat16
EXACT = lax.Precision.HIGHEST
NT = (((1,), (1,)), ((), ()))


def halves(x):
    high = x.astype(BF16)
    return high, (x - high.astype(F32)).astype(BF16)


def dot3(left, right_high, right_low, dims=(((1,), (0,)), ((), ()))):
    rows = left.shape[0]
    high, low = halves(left)
    both = lax.dot_general(
        jnp.concatenate([high, low], 0), right_high, dims, preferred_element_type=F32
    )
    rest = lax.dot_general(high, right_low, dims, preferred_element_type=F32)
    return both[:rows] + (both[rows:] + rest)


def dot_exact(left, right, dims=(((1,), (0,)), ((), ()))):
    return lax.dot_general(left, right, dims, precision=EXACT, preferred_element_type=F32)


def eliminate(systems):
    size, lanes = systems[0].shape
    rows = lax.broadcasted_iota(jnp.int32, (8, lanes), 0)
    tiled = [[system[t : t + 8, :] for t in range(0, size, 8)] for system in systems]
    for k in range(0, size, 4):
        home, first = k // 8, k % 8
        done = []
        for tiles in tiled:
            columns = [
                [jnp.broadcast_to(tile[:, k + j : k + j + 1], (8, lanes)) for tile in tiles] for j in range(4)
            ]
            pivot = [[columns[j][home][first + i : first + i + 1, :] for j in range(4)] for i in range(4)]
            solved = [tiles[home][first + i : first + i + 1, :] for i in range(4)]
            for p in range(4):
                inverse = 1.0 / pivot[p][p]
                solved[p] = solved[p] * inverse
                scaled = [pivot[p][q] * inverse for q in range(p + 1, 4)]
                for i in range(4):
                    if i != p:
                        factor = pivot[i][p]
                        solved[i] = solved[i] - factor * solved[p]
                        for q in range(p + 1, 4):
                            pivot[i][q] = pivot[i][q] - factor * scaled[q - p - 1]
                for q in range(p + 1, 4):
                    pivot[p][q] = scaled[q - p - 1]
            fresh = []
            for t, tile in enumerate(tiles):
                tile = tile - (
                    (columns[0][t] * solved[0] + columns[1][t] * solved[1])
                    + (columns[2][t] * solved[2] + columns[3][t] * solved[3])
                )
                if t == home:
                    for i in range(4):
                        tile = jnp.where(rows == first + i, solved[i], tile)
                fresh.append(tile)
            done.append(fresh)
        tiled = done
    return [jnp.concatenate(tiles, 0) for tiles in tiled]


def total_of(pieces):
    while len(pieces) > 1:
        pieces = [pieces[i] + pieces[i + 1] for i in range(0, len(pieces), 2)]
    return pieces[0]


def fold(both):
    size = both.shape[0]
    row = lax.broadcasted_iota(jnp.int32, both.shape, 0)
    lane = lax.broadcasted_iota(jnp.int32, both.shape, 1)
    second = pltpu.roll(both, size, 1)
    merged = jnp.where(row >= lane, both, second)
    diagonal = jnp.sum(jnp.where(row == lane, second, 0.0), axis=0, keepdims=True)
    top, bottom = merged[: size // 2], pltpu.roll(merged[size // 2 :], size, 1)
    packed = jnp.where(lane[: size // 2] < size, top, bottom)
    return jnp.concatenate([packed, jnp.broadcast_to(diagonal, (8, 2 * size))], 0)


def unfold(packed):
    size = packed.shape[1] // 2
    top = packed[: size // 2]
    merged = jnp.concatenate([top, pltpu.roll(top, size, 1)], 0)[:, :size]
    turned = merged.T
    row = lax.broadcasted_iota(jnp.int32, merged.shape, 0)
    lane = lax.broadcasted_iota(jnp.int32, merged.shape, 1)
    diagonal = jnp.broadcast_to(packed[size // 2 : size // 2 + 1, :size], merged.shape)
    first = jnp.where(row >= lane, merged, turned)
    second = jnp.where(row == lane, diagonal, jnp.where(row < lane, merged, turned))
    return first, second


def kernel(
    obs_ref, order_ref, leaf_ref, factors_ref,
    solution_ref, residual_ref,
    stage, leaf_high, leaf_low, basis_high, basis_low, across_high, across_low,
    gathered, table, picked, order_in, source_in, order_smem, ready,
    r_ref, w_ref, d_ref, s_ref, x_ref, coef_ref, factor_ref,
    c_own, c_in, c_out, c_group, c_all, p_sum, c_sum, y_sum,
    load_sem, smem_sem, order_send, order_recv, near_send, near_recv, far_send, far_recv, back_send, back_recv,
    ring_send, ring_recv, plane_send, plane_recv, coef_send, coef_recv,
):
    group, sub = lax.axis_index("group"), lax.axis_index("sub")
    x = lax.rem(sub, 4)
    z = lax.div(sub, 4)
    core = lax.rem(group, 2)
    y = lax.div(group, 2)
    rhs, points = obs_ref.shape
    rank = factors_ref.shape[0]

    loads = [
        pltpu.make_async_copy(leaf_ref.at[b], stage.at[b], load_sem.at[b]) for b in range(2)
    ]
    for load in loads:
        load.start()

    def on_x(k):
        return (group, z * 4 + (x ^ k))

    def on_z(k):
        return (group, (z ^ k) * 4 + x)

    def on_group(k):
        return (group ^ k, sub)

    def on_plane(k):
        return (group, sub ^ k)

    def on_core(k):
        return (y * 2 + (core ^ k), sub)

    def on_y(k):
        return ((y ^ k) * 2 + core, sub)

    def on_diagonal(j):
        return (group, lax.rem(z + j, 4) * 4 + lax.rem(x + j, 4))

    barrier = pltpu.get_barrier_semaphore()
    for peer in [on_plane(k) for k in range(1, 16)] + [on_group(k) for k in range(1, 8)]:
        pl.semaphore_signal(barrier, inc=1, device_id=peer, device_id_type=MESH)
    pl.semaphore_wait(barrier, 22)

    def remote(source, target, sent, received, peer):
        copy = pltpu.make_async_remote_copy(
            src_ref=source, dst_ref=target, send_sem=sent, recv_sem=received,
            device_id=peer, device_id_type=MESH,
        )
        copy.start()
        return copy

    width = rhs // 8
    by_x, by_z = slice(0, width), slice(width, 2 * width)

    def x_rows(at):
        return pl.ds(pl.multiple_of(at * width, width), width)

    def z_rows(at):
        return pl.ds(pl.multiple_of(rhs // 2 + at * width, width), width)

    order_copies = [
        remote(order_ref, order_in.at[4 - j], order_send.at[j], order_recv.at[4 - j], on_diagonal(j))
        for j in range(1, 4)
    ]
    near = []
    for k in range(1, 4):
        near.append((
            remote(obs_ref.at[x_rows(x ^ k), :], gathered.at[sub, by_x], near_send.at[0, k], near_recv.at[0, k], on_x(k)),
            remote(obs_ref.at[z_rows(z ^ k), :], gathered.at[sub, by_z], near_send.at[1, k], near_recv.at[1, k], on_z(k)),
        ))
    far = []
    for m in range(1, 4):
        far.append(remote(obs_ref.at[x_rows(x), :], gathered.at[sub, by_x], far_send.at[0, 0, m], far_recv.at[0, 0, m], on_z(m)))
        far.append(remote(obs_ref.at[z_rows(z), :], gathered.at[sub, by_z], far_send.at[1, 0, m], far_recv.at[1, 0, m], on_x(m)))
    gathered[sub, by_x, :] = obs_ref[x_rows(x), :]
    gathered[sub, by_z, :] = obs_ref[z_rows(z), :]

    def cut_leaf(b):
        loads[b].wait()

        def cut(i, _):
            rows = pl.ds(pl.multiple_of(i * 64, 64), 64)
            leaf_high[b, rows, :], leaf_low[b, rows, :] = halves(stage[b, rows, :])
            return 0

        lax.fori_loop(0, leaf_ref.shape[1] // 64, cut, 0)

    cut_leaf(0)
    for k in range(1, 4):
        from_x, from_z = near[k - 1]
        from_x.wait()
        slot = gathered.at[z * 4 + (x ^ k), by_x]
        for m in range(1, 4):
            far.append(remote(slot, slot, far_send.at[0, k, m], far_recv.at[0, k, m], on_z(m)))
        from_z.wait()
        slot = gathered.at[(z ^ k) * 4 + x, by_z]
        for m in range(1, 4):
            far.append(remote(slot, slot, far_send.at[1, k, m], far_recv.at[1, k, m], on_x(m)))

    order_in[0] = order_ref[...]
    for copy in order_copies:
        copy.wait()
    for j in range(4):
        position = order_in[j]
        source_in[j] = lax.rem(lax.div(position, points), 8)
        order_in[j] = lax.div(position, points * 8) * points + lax.rem(position, points)
    to_scalar = pltpu.make_async_copy(order_in, order_smem, smem_sem)
    to_scalar.start()
    cut_leaf(1)

    def turn(i, _):
        cols = pl.ds(pl.multiple_of(i * 128, 128), 128)
        part = factors_ref[:, cols]
        basis_high[:, cols], basis_low[:, cols] = halves(part)
        across_high[cols, :], across_low[cols, :] = halves(part.T)
        return 0

    lax.fori_loop(0, points // 128, turn, 0)
    to_scalar.wait()
    for copy in far:
        copy.wait()

    def tabulate(i, _):
        for j in range(4):
            cols = pl.ds(pl.multiple_of(i * 512 + j * 128, 128), 128)
            for h in range(2):
                rows = pl.ds(pl.multiple_of(h * points + i * 512 + j * 128, 128), 128)
                table[rows, :] = gathered[8 * h : 8 * h + 8, :, cols].reshape(128, 128).T
        return 0

    lax.fori_loop(0, points // 512, tabulate, 0)

    back_copies = []
    for j in (2, 1, 3, 0):

        def pick(i, _, j=j):
            for n in range(128):
                picked[pl.ds(i * 128 + n, 1), :] = table[pl.ds(order_smem[j, i, n], 1), :]
            return 0

        lax.fori_loop(0, points // 128, pick, 0)

        def lay(i, _, j=j):
            for n in range(4):
                cols = pl.ds(pl.multiple_of(i * 512 + n * 128, 128), 128)
                turned = picked[cols, :].T
                source = source_in[j, pl.ds(i * 4 + n, 1), :]
                chosen = jnp.where(source == 0, turned[0 : 2 * width], 0.0)
                for g in range(1, 8):
                    chosen = jnp.where(source == g, turned[2 * width * g : 2 * width * (g + 1)], chosen)
                if j:
                    ready[j, :, cols] = chosen
                else:
                    r_ref[0, x_rows(x), cols] = chosen[by_x]
                    r_ref[0, z_rows(z), cols] = chosen[by_z]
            return 0

        lax.fori_loop(0, points // 512, lay, 0)
        if j:
            peer = on_diagonal(j)
            back_copies.append(remote(ready.at[j, by_x], r_ref.at[0, x_rows(x), :], back_send.at[0, j], back_recv.at[0, j], peer))
            back_copies.append(remote(ready.at[j, by_z], r_ref.at[0, z_rows(z), :], back_send.at[1, j], back_recv.at[1, j], peer))
    for copy in back_copies:
        copy.wait()

    def send(kind, turn_at, buffer, slot, peer, count):
        copies = []
        for k in range(1, count):
            copy = pltpu.make_async_remote_copy(
                src_ref=buffer.at[turn_at, slot], dst_ref=buffer.at[turn_at, slot],
                send_sem=ring_send.at[kind, k], recv_sem=ring_recv.at[kind, turn_at, k],
                device_id=peer(k), device_id_type=MESH,
            )
            copy.start()
            copies.append(copy)
        return copies

    def finish(copies):
        for copy in copies:
            copy.wait()

    d_ref[...] = jnp.zeros_like(d_ref)
    s_ref[...] = jnp.zeros_like(s_ref)
    x_ref[...] = jnp.zeros_like(x_ref)
    half = points // 2
    eye = (lax.broadcasted_iota(jnp.int32, (rhs, rhs), 0) == lax.broadcasted_iota(jnp.int32, (rhs, rhs), 1)).astype(F32)

    piece_lane = lax.broadcasted_iota(jnp.int32, (8, 128), 1)

    def by_level(parts):
        return jnp.where(
            piece_lane < 64,
            jnp.where(piece_lane < 32, parts[0], parts[1]),
            jnp.where(piece_lane < 96, parts[2], parts[3]),
        )

    def coef_scatter(at, own):
        for j in range(16):
            c_own[at, j] = own[8 * (j % 8) : 8 * (j % 8) + 8, 128 * (j // 8) : 128 * (j // 8) + 128]
        copies = [
            remote(c_own.at[at, sub ^ k], c_in.at[at, sub], coef_send.at[0, k], coef_recv.at[at, 0, k], on_plane(k))
            for k in FAR_FIRST
        ]
        c_in[at, sub] = c_own[at, sub]
        return copies

    def coef_groups(at, copies):
        finish(copies)
        sums = [[c_in[at, m] for m in range(16)]]
        for _ in range(4):
            sums.append([sums[-1][i] + sums[-1][i + 1] for i in range(0, len(sums[-1]), 2)])
        for m in range(16):
            c_out[at, m] = by_level([sums[level][m >> level] for level in range(4)])
        c_group[at, group] = sums[4][0]
        return [
            remote(c_group.at[at, group], c_group.at[at, group], coef_send.at[1, k], coef_recv.at[at, 1, k], on_group(k))
            for k in (6, 7, 4, 5, 2, 3, 1)
        ]

    def coef_return(at, copies):
        finish(copies)
        own = [c_group[at, group ^ k] for k in range(8)]
        pair = own[0] + own[1]
        four = pair + (own[2] + own[3])
        upper = by_level([own[0], pair, four, four + ((own[4] + own[5]) + (own[6] + own[7]))])
        for m in range(16):
            c_out[at, m] = jnp.where(sub < 8, c_out[at, m], upper)
        copies = [
            remote(c_out.at[at, sub ^ k], c_all.at[at, sub], coef_send.at[2, k], coef_recv.at[at, 2, k], on_plane(k))
            for k in FAR_FIRST
        ]
        c_all[at, sub] = c_out[at, sub]
        return copies

    def coef_whole(at, copies):
        finish(copies)
        return jnp.concatenate(
            [jnp.concatenate([c_all[at, j], c_all[at, j + 8]], 1) for j in range(8)], 0
        )

    def leaf_product(now):
        for b in range(2):
            cols = slice(b * half, (b + 1) * half)
            w_ref[:, cols] = dot3(r_ref[now, :, cols], leaf_high[b], leaf_low[b])

    def weights(matrix):
        high, low = halves(matrix)
        high, low = high.astype(F32), low.astype(F32)
        return jnp.concatenate([high, high, low, low], 0).T.astype(BF16)

    def times(weight, array):
        high, low = halves(array)
        return jnp.dot(
            weight, jnp.concatenate([high, low, high, low], 0), preferred_element_type=F32
        )

    def by_columns(step):
        def body(c, _):
            step(pl.ds(pl.multiple_of(c * 512, 512), 512))
            return 0

        lax.fori_loop(0, points // 512, body, 0)

    def advance_solution(before):
        def step(cols):
            fresh = r_ref[before, :, cols] + times(factor_ref[0], d_ref[:, cols])
            d_ref[:, cols] = fresh
            x_ref[:, cols] = x_ref[:, cols] + times(factor_ref[1], fresh)

        by_columns(step)

    copies = coef_scatter(1, dot3(r_ref[0], across_high[...], across_low[...]))
    leaf_product(0)
    coef_ref[0] = coef_whole(1, coef_return(1, coef_groups(1, copies)))
    coef_ref[1] = jnp.zeros((rhs, rank), F32)
    factor_ref[...] = jnp.zeros_like(factor_ref)

    def iteration(step, carry, more):
        inverse, curv_before = carry
        at = lax.rem(step, 2)
        now, later = at, 1 - at

        for c in range(4):
            cols = slice(c * 512, (c + 1) * 512)
            w_ref[:, cols] = w_ref[:, cols] + dot3(coef_ref[0], basis_high[:, cols], basis_low[:, cols])
        if more:
            copies = coef_scatter(at, dot3(w_ref[...], across_high[...], across_low[...]))

        rw_high, rw_low = halves(jnp.concatenate([r_ref[now], w_ref[...]], 0))
        p_sum[at, sub] = fold(dot3(r_ref[now], rw_high, rw_low, NT))
        sums = [
            remote(p_sum.at[at, sub], p_sum.at[at, sub], plane_send.at[k], plane_recv.at[at, k], on_plane(k))
            for k in FAR_FIRST
        ]
        if more:
            copies = coef_groups(at, copies)

        finish(sums)
        c_sum[at, core] = total_of([p_sum[at, m] for m in range(16)])
        sums = send(5, at, c_sum, core, on_core, 2)
        finish(sums)
        y_sum[at, y] = c_sum[at, 0] + c_sum[at, 1]
        sums = send(7, at, y_sum, y, on_y, 4)

        @pl.when(step > 0)
        def _():
            advance_solution(later)

        if more:
            copies = coef_return(at, copies)
        finish(sums)
        norm, along = unfold(total_of([y_sum[at, m] for m in range(4)]))
        beta = dot_exact(inverse, norm)
        beta_weight = weights(beta)
        factor_ref[0] = beta_weight
        curv = along - dot_exact(beta.T, dot_exact(curv_before, beta))

        def advance(cols):
            s_ref[:, cols] = w_ref[:, cols] + times(beta_weight, s_ref[:, cols])

        by_columns(advance)
        systems = [jnp.concatenate([curv, norm], 1)]
        if more:
            systems.append(jnp.concatenate([norm, eye], 1))
        done = eliminate(systems)
        alpha = done[0][:, rhs:]
        alpha_weight = weights(alpha)
        factor_ref[1] = alpha_weight

        def improve(cols):
            r_ref[later, :, cols] = r_ref[now, :, cols] - times(alpha_weight, s_ref[:, cols])

        by_columns(improve)
        if more:
            coef_ref[1] = coef_whole(at, copies) + dot_exact(beta.T, coef_ref[1])
            coef_ref[0] = coef_ref[0] - dot_exact(alpha.T, coef_ref[1])
            leaf_product(later)
        return done[-1][:, rhs:], curv

    zeros = jnp.zeros((rhs, rhs), F32)
    carry = lax.fori_loop(0, ITERS - 1, functools.partial(iteration, more=True), (zeros, zeros))
    iteration(ITERS - 1, carry, False)
    advance_solution((ITERS - 1) % 2)
    solution_ref[...] = x_ref[...]
    residual_ref[...] = r_ref[ITERS % 2]


def shards(observations, order, leaf_blocks, factors):
    rhs, points = observations.shape
    leaves, leaf = leaf_blocks.shape[:2]
    rank = factors.shape[0] * factors.shape[1]
    vector = pltpu.VMEM((rhs, points), F32)
    dma = pltpu.SemaphoreType.DMA
    vmem = pl.BlockSpec(memory_space=pltpu.VMEM)
    out = jax.ShapeDtypeStruct((rhs, points), F32)
    return pl.pallas_call(
        kernel,
        out_shape=(out, out),
        in_specs=[vmem, vmem, pl.BlockSpec(memory_space=pl.ANY), vmem],
        out_specs=(vmem, vmem),
        scratch_shapes=[
            pltpu.VMEM((leaves, leaf, leaf), F32),
            pltpu.VMEM((leaves, leaf, leaf), BF16),
            pltpu.VMEM((leaves, leaf, leaf), BF16),
            pltpu.VMEM((rank, points), BF16),
            pltpu.VMEM((rank, points), BF16),
            pltpu.VMEM((points, rank), BF16),
            pltpu.VMEM((points, rank), BF16),
            pltpu.VMEM((16, rhs // 4, points), F32),
            pltpu.VMEM((2 * points, 128), F32),
            pltpu.VMEM((points, 128), F32),
            pltpu.VMEM((4, points // 128, 128), jnp.int32),
            pltpu.VMEM((4, points // 128, 128), jnp.int32),
            pltpu.SMEM((4, points // 128, 128), jnp.int32),
            pltpu.VMEM((4, rhs // 4, points), F32),
            pltpu.VMEM((2, rhs, points), F32), vector, vector, vector, vector,
            pltpu.VMEM((2, rhs, rank), F32),
            pltpu.VMEM((2, rhs, 4 * rhs), BF16),
            pltpu.VMEM((2, 16, 8, 128), F32),
            pltpu.VMEM((2, 16, 8, 128), F32),
            pltpu.VMEM((2, 16, 8, 128), F32),
            pltpu.VMEM((2, 8, 8, 128), F32),
            pltpu.VMEM((2, 16, 8, 128), F32),
            pltpu.VMEM((2, 16, rhs // 2 + 8, 2 * rhs), F32),
            pltpu.VMEM((2, 2, rhs // 2 + 8, 2 * rhs), F32),
            pltpu.VMEM((2, 4, rhs // 2 + 8, 2 * rhs), F32),
            dma((2,)), dma, dma((4,)), dma((4,)),
            dma((2, 4)), dma((2, 4)), dma((2, 4, 4)), dma((2, 4, 4)), dma((2, 4)), dma((2, 4)),
            dma((8, 4)), dma((8, 2, 4)), dma((16,)), dma((2, 16)),
            dma((3, 16)), dma((2, 3, 16)),
        ],
        compiler_params=pltpu.CompilerParams(
            collective_id=0, has_side_effects=True, vmem_limit_bytes=60 * 2**20
        ),
        name="block_cg",
    )(observations, order.reshape(points // 128, 128), leaf_blocks, factors.reshape(rank, points))


def solution(mesh):
    in_specs = (
        P(None, ("group", "sub")),
        P(("group", "sub")),
        P(("group", "sub"), None, None),
        P(None, None, ("group", "sub")),
    )
    out_specs = (P(None, ("group", "sub")), P(None, ("group", "sub")))
    return jax.shard_map(shards, mesh=mesh, in_specs=in_specs, out_specs=out_specs, check_vma=False)
```

```python
import functools

import jax
import jax.numpy as jnp
from jax import lax
from jax.experimental import pallas as pl
from jax.experimental.pallas import tpu as pltpu
from jax.sharding import PartitionSpec as P

ITERS = 4
FAR_FIRST = (10, 2, 8, 6, 14, 9, 11, 3, 7, 13, 15, 12, 5, 1, 4)
MESH = pl.DeviceIdType.MESH
F32 = jnp.float32
BF16 = jnp.bfloat16
EXACT = lax.Precision.HIGHEST
NT = (((1,), (1,)), ((), ()))


def halves(x):
    high = x.astype(BF16)
    return high, (x - high.astype(F32)).astype(BF16)


def dot3(left, right_high, right_low, dims=(((1,), (0,)), ((), ()))):
    rows = left.shape[0]
    high, low = halves(left)
    both = lax.dot_general(
        jnp.concatenate([high, low], 0), right_high, dims, preferred_element_type=F32
    )
    rest = lax.dot_general(high, right_low, dims, preferred_element_type=F32)
    return both[:rows] + (both[rows:] + rest)


def dot_exact(left, right, dims=(((1,), (0,)), ((), ()))):
    return lax.dot_general(left, right, dims, precision=EXACT, preferred_element_type=F32)


def eliminate(systems):
    size, lanes = systems[0].shape
    rows = lax.broadcasted_iota(jnp.int32, (8, lanes), 0)
    tiled = [[system[t : t + 8, :] for t in range(0, size, 8)] for system in systems]
    for k in range(0, size, 4):
        home, first = k // 8, k % 8
        done = []
        for tiles in tiled:
            columns = [
                [jnp.broadcast_to(tile[:, k + j : k + j + 1], (8, lanes)) for tile in tiles] for j in range(4)
            ]
            pivot = [[columns[j][home][first + i : first + i + 1, :] for j in range(4)] for i in range(4)]
            solved = [tiles[home][first + i : first + i + 1, :] for i in range(4)]
            for p in range(4):
                inverse = 1.0 / pivot[p][p]
                solved[p] = solved[p] * inverse
                scaled = [pivot[p][q] * inverse for q in range(p + 1, 4)]
                for i in range(4):
                    if i != p:
                        factor = pivot[i][p]
                        solved[i] = solved[i] - factor * solved[p]
                        for q in range(p + 1, 4):
                            pivot[i][q] = pivot[i][q] - factor * scaled[q - p - 1]
                for q in range(p + 1, 4):
                    pivot[p][q] = scaled[q - p - 1]
            fresh = []
            for t, tile in enumerate(tiles):
                tile = tile - (
                    (columns[0][t] * solved[0] + columns[1][t] * solved[1])
                    + (columns[2][t] * solved[2] + columns[3][t] * solved[3])
                )
                if t == home:
                    for i in range(4):
                        tile = jnp.where(rows == first + i, solved[i], tile)
                fresh.append(tile)
            done.append(fresh)
        tiled = done
    return [jnp.concatenate(tiles, 0) for tiles in tiled]


def total_of(pieces):
    while len(pieces) > 1:
        pieces = [pieces[i] + pieces[i + 1] for i in range(0, len(pieces), 2)]
    return pieces[0]


def fold(both):
    size = both.shape[0]
    row = lax.broadcasted_iota(jnp.int32, both.shape, 0)
    lane = lax.broadcasted_iota(jnp.int32, both.shape, 1)
    second = pltpu.roll(both, size, 1)
    merged = jnp.where(row >= lane, both, second)
    diagonal = jnp.sum(jnp.where(row == lane, second, 0.0), axis=0, keepdims=True)
    top, bottom = merged[: size // 2], pltpu.roll(merged[size // 2 :], size, 1)
    packed = jnp.where(lane[: size // 2] < size, top, bottom)
    return jnp.concatenate([packed, jnp.broadcast_to(diagonal, (8, 2 * size))], 0)


def unfold(packed):
    size = packed.shape[1] // 2
    top = packed[: size // 2]
    merged = jnp.concatenate([top, pltpu.roll(top, size, 1)], 0)[:, :size]
    turned = merged.T
    row = lax.broadcasted_iota(jnp.int32, merged.shape, 0)
    lane = lax.broadcasted_iota(jnp.int32, merged.shape, 1)
    diagonal = jnp.broadcast_to(packed[size // 2 : size // 2 + 1, :size], merged.shape)
    first = jnp.where(row >= lane, merged, turned)
    second = jnp.where(row == lane, diagonal, jnp.where(row < lane, merged, turned))
    return first, second


def kernel(
    obs_ref, order_ref, leaf_ref, factors_ref,
    solution_ref, residual_ref,
    stage, leaf_high, leaf_low, basis_high, basis_low, across_high, across_low,
    gathered, table, picked, order_in, source_in, order_smem, ready,
    r_ref, w_ref, d_ref, s_ref, x_ref, coef_ref, factor_ref,
    c_own, c_in, c_out, c_group, c_all, p_sum, c_sum, y_sum,
    load_sem, smem_sem, order_send, order_recv, near_send, near_recv, far_send, far_recv, back_send, back_recv,
    ring_send, ring_recv, plane_send, plane_recv, coef_send, coef_recv,
):
    group, sub = lax.axis_index("group"), lax.axis_index("sub")
    x = lax.rem(sub, 4)
    z = lax.div(sub, 4)
    core = lax.rem(group, 2)
    y = lax.div(group, 2)
    rhs, points = obs_ref.shape
    rank = factors_ref.shape[0]

    loads = [
        pltpu.make_async_copy(leaf_ref.at[b], stage.at[b], load_sem.at[b]) for b in range(2)
    ]
    for load in loads:
        load.start()

    def on_x(k):
        return (group, z * 4 + (x ^ k))

    def on_z(k):
        return (group, (z ^ k) * 4 + x)

    def on_group(k):
        return (group ^ k, sub)

    def on_plane(k):
        return (group, sub ^ k)

    def on_core(k):
        return (y * 2 + (core ^ k), sub)

    def on_y(k):
        return ((y ^ k) * 2 + core, sub)

    def on_diagonal(j):
        return (group, lax.rem(z + j, 4) * 4 + lax.rem(x + j, 4))

    barrier = pltpu.get_barrier_semaphore()
    for peer in [on_plane(k) for k in range(1, 16)] + [on_group(k) for k in range(1, 8)]:
        pl.semaphore_signal(barrier, inc=1, device_id=peer, device_id_type=MESH)
    pl.semaphore_wait(barrier, 22)

    def remote(source, target, sent, received, peer):
        copy = pltpu.make_async_remote_copy(
            src_ref=source, dst_ref=target, send_sem=sent, recv_sem=received,
            device_id=peer, device_id_type=MESH,
        )
        copy.start()
        return copy

    width = rhs // 8
    by_x, by_z = slice(0, width), slice(width, 2 * width)

    def x_rows(at):
        return pl.ds(pl.multiple_of(at * width, width), width)

    def z_rows(at):
        return pl.ds(pl.multiple_of(rhs // 2 + at * width, width), width)

    order_copies = [
        remote(order_ref, order_in.at[4 - j], order_send.at[j], order_recv.at[4 - j], on_diagonal(j))
        for j in range(1, 4)
    ]
    near = []
    for k in range(1, 4):
        near.append((
            remote(obs_ref.at[x_rows(x ^ k), :], gathered.at[sub, by_x], near_send.at[0, k], near_recv.at[0, k], on_x(k)),
            remote(obs_ref.at[z_rows(z ^ k), :], gathered.at[sub, by_z], near_send.at[1, k], near_recv.at[1, k], on_z(k)),
        ))
    far = []
    for m in range(1, 4):
        far.append(remote(obs_ref.at[x_rows(x), :], gathered.at[sub, by_x], far_send.at[0, 0, m], far_recv.at[0, 0, m], on_z(m)))
        far.append(remote(obs_ref.at[z_rows(z), :], gathered.at[sub, by_z], far_send.at[1, 0, m], far_recv.at[1, 0, m], on_x(m)))
    gathered[sub, by_x, :] = obs_ref[x_rows(x), :]
    gathered[sub, by_z, :] = obs_ref[z_rows(z), :]

    def cut_leaf(b):
        loads[b].wait()

        def cut(i, _):
            rows = pl.ds(pl.multiple_of(i * 64, 64), 64)
            leaf_high[b, rows, :], leaf_low[b, rows, :] = halves(stage[b, rows, :])
            return 0

        lax.fori_loop(0, leaf_ref.shape[1] // 64, cut, 0)

    cut_leaf(0)
    for k in range(1, 4):
        from_x, from_z = near[k - 1]
        from_x.wait()
        slot = gathered.at[z * 4 + (x ^ k), by_x]
        for m in range(1, 4):
            far.append(remote(slot, slot, far_send.at[0, k, m], far_recv.at[0, k, m], on_z(m)))
        from_z.wait()
        slot = gathered.at[(z ^ k) * 4 + x, by_z]
        for m in range(1, 4):
            far.append(remote(slot, slot, far_send.at[1, k, m], far_recv.at[1, k, m], on_x(m)))

    order_in[0] = order_ref[...]
    for copy in order_copies:
        copy.wait()
    for j in range(4):
        position = order_in[j]
        source_in[j] = lax.rem(lax.div(position, points), 8)
        order_in[j] = lax.div(position, points * 8) * points + lax.rem(position, points)
    to_scalar = pltpu.make_async_copy(order_in, order_smem, smem_sem)
    to_scalar.start()
    cut_leaf(1)

    def turn(i, _):
        cols = pl.ds(pl.multiple_of(i * 128, 128), 128)
        part = factors_ref[:, cols]
        basis_high[:, cols], basis_low[:, cols] = halves(part)
        across_high[cols, :], across_low[cols, :] = halves(part.T)
        return 0

    lax.fori_loop(0, points // 128, turn, 0)
    to_scalar.wait()
    for copy in far:
        copy.wait()

    def tabulate(i, _):
        for j in range(4):
            cols = pl.ds(pl.multiple_of(i * 512 + j * 128, 128), 128)
            for h in range(2):
                rows = pl.ds(pl.multiple_of(h * points + i * 512 + j * 128, 128), 128)
                table[rows, :] = gathered[8 * h : 8 * h + 8, :, cols].reshape(128, 128).T
        return 0

    lax.fori_loop(0, points // 512, tabulate, 0)

    back_copies = []
    for j in (2, 1, 3, 0):

        def pick(i, _, j=j):
            for n in range(128):
                picked[pl.ds(i * 128 + n, 1), :] = table[pl.ds(order_smem[j, i, n], 1), :]
            return 0

        lax.fori_loop(0, points // 128, pick, 0)

        def lay(i, _, j=j):
            for n in range(4):
                cols = pl.ds(pl.multiple_of(i * 512 + n * 128, 128), 128)
                turned = picked[cols, :].T
                source = source_in[j, pl.ds(i * 4 + n, 1), :]
                chosen = jnp.where(source == 0, turned[0 : 2 * width], 0.0)
                for g in range(1, 8):
                    chosen = jnp.where(source == g, turned[2 * width * g : 2 * width * (g + 1)], chosen)
                if j:
                    ready[j, :, cols] = chosen
                else:
                    r_ref[0, x_rows(x), cols] = chosen[by_x]
                    r_ref[0, z_rows(z), cols] = chosen[by_z]
            return 0

        lax.fori_loop(0, points // 512, lay, 0)
        if j:
            peer = on_diagonal(j)
            back_copies.append(remote(ready.at[j, by_x], r_ref.at[0, x_rows(x), :], back_send.at[0, j], back_recv.at[0, j], peer))
            back_copies.append(remote(ready.at[j, by_z], r_ref.at[0, z_rows(z), :], back_send.at[1, j], back_recv.at[1, j], peer))
    for copy in back_copies:
        copy.wait()

    def send(kind, turn_at, buffer, slot, peer, count):
        copies = []
        for k in range(1, count):
            copy = pltpu.make_async_remote_copy(
                src_ref=buffer.at[turn_at, slot], dst_ref=buffer.at[turn_at, slot],
                send_sem=ring_send.at[kind, k], recv_sem=ring_recv.at[kind, turn_at, k],
                device_id=peer(k), device_id_type=MESH,
            )
            copy.start()
            copies.append(copy)
        return copies

    def finish(copies):
        for copy in copies:
            copy.wait()

    d_ref[...] = jnp.zeros_like(d_ref)
    s_ref[...] = jnp.zeros_like(s_ref)
    x_ref[...] = jnp.zeros_like(x_ref)
    half = points // 2
    eye = (lax.broadcasted_iota(jnp.int32, (rhs, rhs), 0) == lax.broadcasted_iota(jnp.int32, (rhs, rhs), 1)).astype(F32)

    piece_lane = lax.broadcasted_iota(jnp.int32, (8, 128), 1)

    def by_level(parts):
        return jnp.where(
            piece_lane < 64,
            jnp.where(piece_lane < 32, parts[0], parts[1]),
            jnp.where(piece_lane < 96, parts[2], parts[3]),
        )

    def coef_scatter(at, own):
        for j in range(16):
            c_own[at, j] = own[8 * (j % 8) : 8 * (j % 8) + 8, 128 * (j // 8) : 128 * (j // 8) + 128]
        copies = [
            remote(c_own.at[at, sub ^ k], c_in.at[at, sub], coef_send.at[0, k], coef_recv.at[at, 0, k], on_plane(k))
            for k in FAR_FIRST
        ]
        c_in[at, sub] = c_own[at, sub]
        return copies

    def coef_groups(at, copies):
        finish(copies)
        sums = [[c_in[at, m] for m in range(16)]]
        for _ in range(4):
            sums.append([sums[-1][i] + sums[-1][i + 1] for i in range(0, len(sums[-1]), 2)])
        for m in range(16):
            c_out[at, m] = by_level([sums[level][m >> level] for level in range(4)])
        c_group[at, group] = sums[4][0]
        return [
            remote(c_group.at[at, group], c_group.at[at, group], coef_send.at[1, k], coef_recv.at[at, 1, k], on_group(k))
            for k in (6, 7, 4, 5, 2, 3, 1)
        ]

    def coef_return(at, copies):
        finish(copies)
        own = [c_group[at, group ^ k] for k in range(8)]
        pair = own[0] + own[1]
        four = pair + (own[2] + own[3])
        upper = by_level([own[0], pair, four, four + ((own[4] + own[5]) + (own[6] + own[7]))])
        for m in range(16):
            c_out[at, m] = jnp.where(sub < 8, c_out[at, m], upper)
        copies = [
            remote(c_out.at[at, sub ^ k], c_all.at[at, sub], coef_send.at[2, k], coef_recv.at[at, 2, k], on_plane(k))
            for k in FAR_FIRST
        ]
        c_all[at, sub] = c_out[at, sub]
        return copies

    def coef_whole(at, copies):
        finish(copies)
        return jnp.concatenate(
            [jnp.concatenate([c_all[at, j], c_all[at, j + 8]], 1) for j in range(8)], 0
        )

    def leaf_product(now):
        for b in range(2):
            cols = slice(b * half, (b + 1) * half)
            w_ref[:, cols] = dot3(r_ref[now, :, cols], leaf_high[b], leaf_low[b])

    def weights(matrix):
        high, low = halves(matrix)
        high, low = high.astype(F32), low.astype(F32)
        return jnp.concatenate([high, high, low, low], 0).T.astype(BF16)

    def times(weight, array):
        high, low = halves(array)
        return jnp.dot(
            weight, jnp.concatenate([high, low, high, low], 0), preferred_element_type=F32
        )

    def by_columns(step):
        def body(c, _):
            step(pl.ds(pl.multiple_of(c * 512, 512), 512))
            return 0

        lax.fori_loop(0, points // 512, body, 0)

    def advance_solution(before):
        def step(cols):
            fresh = r_ref[before, :, cols] + times(factor_ref[0], d_ref[:, cols])
            d_ref[:, cols] = fresh
            x_ref[:, cols] = x_ref[:, cols] + times(factor_ref[1], fresh)

        by_columns(step)

    copies = coef_scatter(1, dot3(r_ref[0], across_high[...], across_low[...]))
    leaf_product(0)
    coef_ref[0] = coef_whole(1, coef_return(1, coef_groups(1, copies)))
    coef_ref[1] = jnp.zeros((rhs, rank), F32)
    factor_ref[...] = jnp.zeros_like(factor_ref)

    def iteration(step, carry, more):
        inverse, curv_before = carry
        at = lax.rem(step, 2)
        now, later = at, 1 - at

        for c in range(4):
            cols = slice(c * 512, (c + 1) * 512)
            w_ref[:, cols] = w_ref[:, cols] + dot3(coef_ref[0], basis_high[:, cols], basis_low[:, cols])
        rw_high, rw_low = halves(jnp.concatenate([r_ref[now], w_ref[...]], 0))
        p_sum[at, sub] = fold(dot3(r_ref[now], rw_high, rw_low, NT))
        sums = [
            remote(p_sum.at[at, sub], p_sum.at[at, sub], plane_send.at[k], plane_recv.at[at, k], on_plane(k))
            for k in FAR_FIRST
        ]
        if more:
            copies = coef_scatter(at, dot3(w_ref[...], across_high[...], across_low[...]))

        finish(sums)
        c_sum[at, core] = total_of([p_sum[at, m] for m in range(16)])
        sums = send(5, at, c_sum, core, on_core, 2)
        if more:
            copies = coef_groups(at, copies)

        finish(sums)
        y_sum[at, y] = c_sum[at, 0] + c_sum[at, 1]
        sums = send(7, at, y_sum, y, on_y, 4)

        @pl.when(step > 0)
        def _():
            advance_solution(later)

        if more:
            copies = coef_return(at, copies)
        finish(sums)
        norm, along = unfold(total_of([y_sum[at, m] for m in range(4)]))
        beta = dot_exact(inverse, norm)
        beta_weight = weights(beta)
        factor_ref[0] = beta_weight
        curv = along - dot_exact(beta.T, dot_exact(curv_before, beta))

        def advance(cols):
            s_ref[:, cols] = w_ref[:, cols] + times(beta_weight, s_ref[:, cols])

        by_columns(advance)
        systems = [jnp.concatenate([curv, norm], 1)]
        if more:
            systems.append(jnp.concatenate([norm, eye], 1))
        done = eliminate(systems)
        alpha = done[0][:, rhs:]
        alpha_weight = weights(alpha)
        factor_ref[1] = alpha_weight

        def improve(cols):
            r_ref[later, :, cols] = r_ref[now, :, cols] - times(alpha_weight, s_ref[:, cols])

        by_columns(improve)
        if more:
            coef_ref[1] = coef_whole(at, copies) + dot_exact(beta.T, coef_ref[1])
            coef_ref[0] = coef_ref[0] - dot_exact(alpha.T, coef_ref[1])
            leaf_product(later)
        return done[-1][:, rhs:], curv

    zeros = jnp.zeros((rhs, rhs), F32)
    carry = lax.fori_loop(0, ITERS - 1, functools.partial(iteration, more=True), (zeros, zeros))
    iteration(ITERS - 1, carry, False)
    advance_solution((ITERS - 1) % 2)
    solution_ref[...] = x_ref[...]
    residual_ref[...] = r_ref[ITERS % 2]


def shards(observations, order, leaf_blocks, factors):
    rhs, points = observations.shape
    leaves, leaf = leaf_blocks.shape[:2]
    rank = factors.shape[0] * factors.shape[1]
    vector = pltpu.VMEM((rhs, points), F32)
    dma = pltpu.SemaphoreType.DMA
    vmem = pl.BlockSpec(memory_space=pltpu.VMEM)
    out = jax.ShapeDtypeStruct((rhs, points), F32)
    return pl.pallas_call(
        kernel,
        out_shape=(out, out),
        in_specs=[vmem, vmem, pl.BlockSpec(memory_space=pl.ANY), vmem],
        out_specs=(vmem, vmem),
        scratch_shapes=[
            pltpu.VMEM((leaves, leaf, leaf), F32),
            pltpu.VMEM((leaves, leaf, leaf), BF16),
            pltpu.VMEM((leaves, leaf, leaf), BF16),
            pltpu.VMEM((rank, points), BF16),
            pltpu.VMEM((rank, points), BF16),
            pltpu.VMEM((points, rank), BF16),
            pltpu.VMEM((points, rank), BF16),
            pltpu.VMEM((16, rhs // 4, points), F32),
            pltpu.VMEM((2 * points, 128), F32),
            pltpu.VMEM((points, 128), F32),
            pltpu.VMEM((4, points // 128, 128), jnp.int32),
            pltpu.VMEM((4, points // 128, 128), jnp.int32),
            pltpu.SMEM((4, points // 128, 128), jnp.int32),
            pltpu.VMEM((4, rhs // 4, points), F32),
            pltpu.VMEM((2, rhs, points), F32), vector, vector, vector, vector,
            pltpu.VMEM((2, rhs, rank), F32),
            pltpu.VMEM((2, rhs, 4 * rhs), BF16),
            pltpu.VMEM((2, 16, 8, 128), F32),
            pltpu.VMEM((2, 16, 8, 128), F32),
            pltpu.VMEM((2, 16, 8, 128), F32),
            pltpu.VMEM((2, 8, 8, 128), F32),
            pltpu.VMEM((2, 16, 8, 128), F32),
            pltpu.VMEM((2, 16, rhs // 2 + 8, 2 * rhs), F32),
            pltpu.VMEM((2, 2, rhs // 2 + 8, 2 * rhs), F32),
            pltpu.VMEM((2, 4, rhs // 2 + 8, 2 * rhs), F32),
            dma((2,)), dma, dma((4,)), dma((4,)),
            dma((2, 4)), dma((2, 4)), dma((2, 4, 4)), dma((2, 4, 4)), dma((2, 4)), dma((2, 4)),
            dma((8, 4)), dma((8, 2, 4)), dma((16,)), dma((2, 16)),
            dma((3, 16)), dma((2, 3, 16)),
        ],
        compiler_params=pltpu.CompilerParams(
            collective_id=0, has_side_effects=True, vmem_limit_bytes=60 * 2**20
        ),
        name="block_cg",
    )(observations, order.reshape(points // 128, 128), leaf_blocks, factors.reshape(rank, points))


def solution(mesh):
    in_specs = (
        P(None, ("group", "sub")),
        P(("group", "sub")),
        P(("group", "sub"), None, None),
        P(None, None, ("group", "sub")),
    )
    out_specs = (P(None, ("group", "sub")), P(None, ("group", "sub")))
    return jax.shard_map(shards, mesh=mesh, in_specs=in_specs, out_specs=out_specs, check_vma=False)
```

```python
import functools

import jax
import jax.numpy as jnp
from jax import lax
from jax.experimental import pallas as pl
from jax.experimental.pallas import tpu as pltpu
from jax.sharding import PartitionSpec as P

ITERS = 4
FAR_FIRST = (10, 2, 8, 6, 14, 9, 11, 3, 7, 13, 15, 12, 5, 1, 4)
MESH = pl.DeviceIdType.MESH
F32 = jnp.float32
BF16 = jnp.bfloat16
EXACT = lax.Precision.HIGHEST
NT = (((1,), (1,)), ((), ()))


def halves(x):
    high = x.astype(BF16)
    return high, (x - high.astype(F32)).astype(BF16)


def dot3(left, right_high, right_low, dims=(((1,), (0,)), ((), ()))):
    rows = left.shape[0]
    high, low = halves(left)
    both = lax.dot_general(
        jnp.concatenate([high, low], 0), right_high, dims, preferred_element_type=F32
    )
    rest = lax.dot_general(high, right_low, dims, preferred_element_type=F32)
    return both[:rows] + (both[rows:] + rest)


def dot_exact(left, right, dims=(((1,), (0,)), ((), ()))):
    return lax.dot_general(left, right, dims, precision=EXACT, preferred_element_type=F32)


def eliminate(systems):
    size, lanes = systems[0].shape
    rows = lax.broadcasted_iota(jnp.int32, (8, lanes), 0)
    tiled = [[system[t : t + 8, :] for t in range(0, size, 8)] for system in systems]
    for k in range(0, size, 4):
        home, first = k // 8, k % 8
        done = []
        for tiles in tiled:
            columns = [
                [jnp.broadcast_to(tile[:, k + j : k + j + 1], (8, lanes)) for tile in tiles] for j in range(4)
            ]
            pivot = [[columns[j][home][first + i : first + i + 1, :] for j in range(4)] for i in range(4)]
            solved = [tiles[home][first + i : first + i + 1, :] for i in range(4)]
            for p in range(4):
                inverse = 1.0 / pivot[p][p]
                solved[p] = solved[p] * inverse
                scaled = [pivot[p][q] * inverse for q in range(p + 1, 4)]
                for i in range(4):
                    if i != p:
                        factor = pivot[i][p]
                        solved[i] = solved[i] - factor * solved[p]
                        for q in range(p + 1, 4):
                            pivot[i][q] = pivot[i][q] - factor * scaled[q - p - 1]
                for q in range(p + 1, 4):
                    pivot[p][q] = scaled[q - p - 1]
            fresh = []
            for t, tile in enumerate(tiles):
                tile = tile - (
                    (columns[0][t] * solved[0] + columns[1][t] * solved[1])
                    + (columns[2][t] * solved[2] + columns[3][t] * solved[3])
                )
                if t == home:
                    for i in range(4):
                        tile = jnp.where(rows == first + i, solved[i], tile)
                fresh.append(tile)
            done.append(fresh)
        tiled = done
    return [jnp.concatenate(tiles, 0) for tiles in tiled]


def total_of(pieces):
    while len(pieces) > 1:
        pieces = [pieces[i] + pieces[i + 1] for i in range(0, len(pieces), 2)]
    return pieces[0]


def fold(both):
    size = both.shape[0]
    row = lax.broadcasted_iota(jnp.int32, both.shape, 0)
    lane = lax.broadcasted_iota(jnp.int32, both.shape, 1)
    second = pltpu.roll(both, size, 1)
    merged = jnp.where(row >= lane, both, second)
    diagonal = jnp.sum(jnp.where(row == lane, second, 0.0), axis=0, keepdims=True)
    top, bottom = merged[: size // 2], pltpu.roll(merged[size // 2 :], size, 1)
    packed = jnp.where(lane[: size // 2] < size, top, bottom)
    return jnp.concatenate([packed, jnp.broadcast_to(diagonal, (8, 2 * size))], 0)


def unfold(packed):
    size = packed.shape[1] // 2
    top = packed[: size // 2]
    merged = jnp.concatenate([top, pltpu.roll(top, size, 1)], 0)[:, :size]
    turned = merged.T
    row = lax.broadcasted_iota(jnp.int32, merged.shape, 0)
    lane = lax.broadcasted_iota(jnp.int32, merged.shape, 1)
    diagonal = jnp.broadcast_to(packed[size // 2 : size // 2 + 1, :size], merged.shape)
    first = jnp.where(row >= lane, merged, turned)
    second = jnp.where(row == lane, diagonal, jnp.where(row < lane, merged, turned))
    return first, second


def kernel(
    obs_far, order_far, leaf_ref, factors_far,
    solution_ref, residual_ref,
    obs_ref, order_ref, factors_ref, stage, leaf_high, leaf_low, basis_high, basis_low, across_high, across_low,
    gathered, table, picked, order_in, source_in, order_smem, ready,
    r_ref, w_ref, d_ref, s_ref, x_ref, coef_ref, factor_ref,
    c_own, c_in, c_out, c_group, c_all, p_sum, c_sum, y_sum,
    load_sem, smem_sem, order_send, order_recv, near_send, near_recv, far_send, far_recv, back_send, back_recv,
    ring_send, ring_recv, plane_send, plane_recv, coef_send, coef_recv,
):
    group, sub = lax.axis_index("group"), lax.axis_index("sub")
    x = lax.rem(sub, 4)
    z = lax.div(sub, 4)
    core = lax.rem(group, 2)
    y = lax.div(group, 2)
    rhs, points = obs_ref.shape
    rank = factors_ref.shape[0]

    obs_load = pltpu.make_async_copy(obs_far, obs_ref, load_sem.at[2])
    order_load = pltpu.make_async_copy(order_far, order_ref, load_sem.at[3])
    factors_load = pltpu.make_async_copy(factors_far, factors_ref, load_sem.at[4])
    loads = [
        pltpu.make_async_copy(leaf_ref.at[b], stage.at[b], load_sem.at[b]) for b in range(2)
    ]
    for load in [order_load, obs_load, *loads, factors_load]:
        load.start()

    def on_x(k):
        return (group, z * 4 + (x ^ k))

    def on_z(k):
        return (group, (z ^ k) * 4 + x)

    def on_group(k):
        return (group ^ k, sub)

    def on_plane(k):
        return (group, sub ^ k)

    def on_core(k):
        return (y * 2 + (core ^ k), sub)

    def on_y(k):
        return ((y ^ k) * 2 + core, sub)

    def on_diagonal(j):
        return (group, lax.rem(z + j, 4) * 4 + lax.rem(x + j, 4))

    barrier = pltpu.get_barrier_semaphore()
    for peer in [on_plane(k) for k in range(1, 16)] + [on_group(k) for k in range(1, 8)]:
        pl.semaphore_signal(barrier, inc=1, device_id=peer, device_id_type=MESH)
    order_load.wait()
    obs_load.wait()
    pl.semaphore_wait(barrier, 22)

    def remote(source, target, sent, received, peer):
        copy = pltpu.make_async_remote_copy(
            src_ref=source, dst_ref=target, send_sem=sent, recv_sem=received,
            device_id=peer, device_id_type=MESH,
        )
        copy.start()
        return copy

    width = rhs // 8
    by_x, by_z = slice(0, width), slice(width, 2 * width)

    def x_rows(at):
        return pl.ds(pl.multiple_of(at * width, width), width)

    def z_rows(at):
        return pl.ds(pl.multiple_of(rhs // 2 + at * width, width), width)

    order_copies = [
        remote(order_ref, order_in.at[4 - j], order_send.at[j], order_recv.at[4 - j], on_diagonal(j))
        for j in range(1, 4)
    ]
    near = []
    for k in range(1, 4):
        near.append((
            remote(obs_ref.at[x_rows(x ^ k), :], gathered.at[sub, by_x], near_send.at[0, k], near_recv.at[0, k], on_x(k)),
            remote(obs_ref.at[z_rows(z ^ k), :], gathered.at[sub, by_z], near_send.at[1, k], near_recv.at[1, k], on_z(k)),
        ))
    far = []
    for m in range(1, 4):
        far.append(remote(obs_ref.at[x_rows(x), :], gathered.at[sub, by_x], far_send.at[0, 0, m], far_recv.at[0, 0, m], on_z(m)))
        far.append(remote(obs_ref.at[z_rows(z), :], gathered.at[sub, by_z], far_send.at[1, 0, m], far_recv.at[1, 0, m], on_x(m)))
    gathered[sub, by_x, :] = obs_ref[x_rows(x), :]
    gathered[sub, by_z, :] = obs_ref[z_rows(z), :]

    def cut_leaf(b):
        loads[b].wait()

        def cut(i, _):
            rows = pl.ds(pl.multiple_of(i * 64, 64), 64)
            leaf_high[b, rows, :], leaf_low[b, rows, :] = halves(stage[b, rows, :])
            return 0

        lax.fori_loop(0, leaf_ref.shape[1] // 64, cut, 0)

    cut_leaf(0)
    for k in range(1, 4):
        from_x, from_z = near[k - 1]
        from_x.wait()
        slot = gathered.at[z * 4 + (x ^ k), by_x]
        for m in range(1, 4):
            far.append(remote(slot, slot, far_send.at[0, k, m], far_recv.at[0, k, m], on_z(m)))
        from_z.wait()
        slot = gathered.at[(z ^ k) * 4 + x, by_z]
        for m in range(1, 4):
            far.append(remote(slot, slot, far_send.at[1, k, m], far_recv.at[1, k, m], on_x(m)))

    order_in[0] = order_ref[...]
    for copy in order_copies:
        copy.wait()
    for j in range(4):
        position = order_in[j]
        source_in[j] = lax.rem(lax.div(position, points), 8)
        order_in[j] = lax.div(position, points * 8) * points + lax.rem(position, points)
    to_scalar = pltpu.make_async_copy(order_in, order_smem, smem_sem)
    to_scalar.start()
    cut_leaf(1)

    def turn(i, _):
        cols = pl.ds(pl.multiple_of(i * 128, 128), 128)
        part = factors_ref[:, cols]
        basis_high[:, cols], basis_low[:, cols] = halves(part)
        across_high[cols, :], across_low[cols, :] = halves(part.T)
        return 0

    factors_load.wait()
    lax.fori_loop(0, points // 128, turn, 0)
    to_scalar.wait()
    for copy in far:
        copy.wait()

    def tabulate(i, _):
        for j in range(4):
            cols = pl.ds(pl.multiple_of(i * 512 + j * 128, 128), 128)
            for h in range(2):
                rows = pl.ds(pl.multiple_of(h * points + i * 512 + j * 128, 128), 128)
                table[rows, :] = gathered[8 * h : 8 * h + 8, :, cols].reshape(128, 128).T
        return 0

    lax.fori_loop(0, points // 512, tabulate, 0)

    back_copies = []
    for j in (2, 1, 3, 0):

        def pick(i, _, j=j):
            for n in range(128):
                picked[pl.ds(i * 128 + n, 1), :] = table[pl.ds(order_smem[j, i, n], 1), :]
            return 0

        lax.fori_loop(0, points // 128, pick, 0)

        def lay(i, _, j=j):
            for n in range(4):
                cols = pl.ds(pl.multiple_of(i * 512 + n * 128, 128), 128)
                turned = picked[cols, :].T
                source = source_in[j, pl.ds(i * 4 + n, 1), :]
                chosen = jnp.where(source == 0, turned[0 : 2 * width], 0.0)
                for g in range(1, 8):
                    chosen = jnp.where(source == g, turned[2 * width * g : 2 * width * (g + 1)], chosen)
                if j:
                    ready[j, :, cols] = chosen
                else:
                    r_ref[0, x_rows(x), cols] = chosen[by_x]
                    r_ref[0, z_rows(z), cols] = chosen[by_z]
            return 0

        lax.fori_loop(0, points // 512, lay, 0)
        if j:
            peer = on_diagonal(j)
            back_copies.append(remote(ready.at[j, by_x], r_ref.at[0, x_rows(x), :], back_send.at[0, j], back_recv.at[0, j], peer))
            back_copies.append(remote(ready.at[j, by_z], r_ref.at[0, z_rows(z), :], back_send.at[1, j], back_recv.at[1, j], peer))
    for copy in back_copies:
        copy.wait()

    def send(kind, turn_at, buffer, slot, peer, count):
        copies = []
        for k in range(1, count):
            copy = pltpu.make_async_remote_copy(
                src_ref=buffer.at[turn_at, slot], dst_ref=buffer.at[turn_at, slot],
                send_sem=ring_send.at[kind, k], recv_sem=ring_recv.at[kind, turn_at, k],
                device_id=peer(k), device_id_type=MESH,
            )
            copy.start()
            copies.append(copy)
        return copies

    def finish(copies):
        for copy in copies:
            copy.wait()

    d_ref[...] = jnp.zeros_like(d_ref)
    s_ref[...] = jnp.zeros_like(s_ref)
    x_ref[...] = jnp.zeros_like(x_ref)
    half = points // 2
    eye = (lax.broadcasted_iota(jnp.int32, (rhs, rhs), 0) == lax.broadcasted_iota(jnp.int32, (rhs, rhs), 1)).astype(F32)

    piece_lane = lax.broadcasted_iota(jnp.int32, (8, 128), 1)

    def by_level(parts):
        return jnp.where(
            piece_lane < 64,
            jnp.where(piece_lane < 32, parts[0], parts[1]),
            jnp.where(piece_lane < 96, parts[2], parts[3]),
        )

    def coef_scatter(at, own):
        for j in range(16):
            c_own[at, j] = own[8 * (j % 8) : 8 * (j % 8) + 8, 128 * (j // 8) : 128 * (j // 8) + 128]
        copies = [
            remote(c_own.at[at, sub ^ k], c_in.at[at, sub], coef_send.at[0, k], coef_recv.at[at, 0, k], on_plane(k))
            for k in FAR_FIRST
        ]
        c_in[at, sub] = c_own[at, sub]
        return copies

    def coef_groups(at, copies):
        finish(copies)
        sums = [[c_in[at, m] for m in range(16)]]
        for _ in range(4):
            sums.append([sums[-1][i] + sums[-1][i + 1] for i in range(0, len(sums[-1]), 2)])
        for m in range(16):
            c_out[at, m] = by_level([sums[level][m >> level] for level in range(4)])
        c_group[at, group] = sums[4][0]
        return [
            remote(c_group.at[at, group], c_group.at[at, group], coef_send.at[1, k], coef_recv.at[at, 1, k], on_group(k))
            for k in (6, 7, 4, 5, 2, 3, 1)
        ]

    def coef_return(at, copies):
        finish(copies)
        own = [c_group[at, group ^ k] for k in range(8)]
        pair = own[0] + own[1]
        four = pair + (own[2] + own[3])
        upper = by_level([own[0], pair, four, four + ((own[4] + own[5]) + (own[6] + own[7]))])
        for m in range(16):
            c_out[at, m] = jnp.where(sub < 8, c_out[at, m], upper)
        copies = [
            remote(c_out.at[at, sub ^ k], c_all.at[at, sub], coef_send.at[2, k], coef_recv.at[at, 2, k], on_plane(k))
            for k in FAR_FIRST
        ]
        c_all[at, sub] = c_out[at, sub]
        return copies

    def coef_whole(at, copies):
        finish(copies)
        return jnp.concatenate(
            [jnp.concatenate([c_all[at, j], c_all[at, j + 8]], 1) for j in range(8)], 0
        )

    def leaf_product(now):
        for b in range(2):
            cols = slice(b * half, (b + 1) * half)
            w_ref[:, cols] = dot3(r_ref[now, :, cols], leaf_high[b], leaf_low[b])

    def weights(matrix):
        high, low = halves(matrix)
        high, low = high.astype(F32), low.astype(F32)
        return jnp.concatenate([high, high, low, low], 0).T.astype(BF16)

    def times(weight, array):
        high, low = halves(array)
        return jnp.dot(
            weight, jnp.concatenate([high, low, high, low], 0), preferred_element_type=F32
        )

    def by_columns(step):
        def body(c, _):
            step(pl.ds(pl.multiple_of(c * 512, 512), 512))
            return 0

        lax.fori_loop(0, points // 512, body, 0)

    def advance_solution(before):
        def step(cols):
            fresh = r_ref[before, :, cols] + times(factor_ref[0], d_ref[:, cols])
            d_ref[:, cols] = fresh
            x_ref[:, cols] = x_ref[:, cols] + times(factor_ref[1], fresh)

        by_columns(step)

    copies = coef_scatter(1, dot3(r_ref[0], across_high[...], across_low[...]))
    leaf_product(0)
    coef_ref[0] = coef_whole(1, coef_return(1, coef_groups(1, copies)))
    coef_ref[1] = jnp.zeros((rhs, rank), F32)
    factor_ref[...] = jnp.zeros_like(factor_ref)

    def iteration(step, carry, more):
        inverse, curv_before = carry
        at = lax.rem(step, 2)
        now, later = at, 1 - at

        for c in range(4):
            cols = slice(c * 512, (c + 1) * 512)
            w_ref[:, cols] = w_ref[:, cols] + dot3(coef_ref[0], basis_high[:, cols], basis_low[:, cols])
        rw_high, rw_low = halves(jnp.concatenate([r_ref[now], w_ref[...]], 0))
        p_sum[at, sub] = fold(dot3(r_ref[now], rw_high, rw_low, NT))
        sums = [
            remote(p_sum.at[at, sub], p_sum.at[at, sub], plane_send.at[k], plane_recv.at[at, k], on_plane(k))
            for k in FAR_FIRST
        ]
        if more:
            copies = coef_scatter(at, dot3(w_ref[...], across_high[...], across_low[...]))

        finish(sums)
        c_sum[at, core] = total_of([p_sum[at, m] for m in range(16)])
        sums = send(5, at, c_sum, core, on_core, 2)
        if more:
            copies = coef_groups(at, copies)

        finish(sums)
        y_sum[at, y] = c_sum[at, 0] + c_sum[at, 1]
        sums = send(7, at, y_sum, y, on_y, 4)

        @pl.when(step > 0)
        def _():
            advance_solution(later)

        if more:
            copies = coef_return(at, copies)
        finish(sums)
        norm, along = unfold(total_of([y_sum[at, m] for m in range(4)]))
        beta = dot_exact(inverse, norm)
        beta_weight = weights(beta)
        factor_ref[0] = beta_weight
        curv = along - dot_exact(beta.T, dot_exact(curv_before, beta))

        def advance(cols):
            s_ref[:, cols] = w_ref[:, cols] + times(beta_weight, s_ref[:, cols])

        by_columns(advance)
        systems = [jnp.concatenate([curv, norm], 1)]
        if more:
            systems.append(jnp.concatenate([norm, eye], 1))
        done = eliminate(systems)
        alpha = done[0][:, rhs:]
        alpha_weight = weights(alpha)
        factor_ref[1] = alpha_weight

        def improve(cols):
            r_ref[later, :, cols] = r_ref[now, :, cols] - times(alpha_weight, s_ref[:, cols])

        by_columns(improve)
        if more:
            coef_ref[1] = coef_whole(at, copies) + dot_exact(beta.T, coef_ref[1])
            coef_ref[0] = coef_ref[0] - dot_exact(alpha.T, coef_ref[1])
            leaf_product(later)
        return done[-1][:, rhs:], curv

    zeros = jnp.zeros((rhs, rhs), F32)
    carry = lax.fori_loop(0, ITERS - 1, functools.partial(iteration, more=True), (zeros, zeros))
    iteration(ITERS - 1, carry, False)
    residual_out = pltpu.make_async_copy(r_ref.at[ITERS % 2], residual_ref, load_sem.at[0])
    residual_out.start()
    advance_solution((ITERS - 1) % 2)
    solution_out = pltpu.make_async_copy(x_ref, solution_ref, load_sem.at[1])
    solution_out.start()
    residual_out.wait()
    solution_out.wait()


def shards(observations, order, leaf_blocks, factors):
    rhs, points = observations.shape
    leaves, leaf = leaf_blocks.shape[:2]
    rank = factors.shape[0] * factors.shape[1]
    vector = pltpu.VMEM((rhs, points), F32)
    dma = pltpu.SemaphoreType.DMA
    anywhere = pl.BlockSpec(memory_space=pl.ANY)
    out = jax.ShapeDtypeStruct((rhs, points), F32)
    return pl.pallas_call(
        kernel,
        out_shape=(out, out),
        in_specs=[anywhere] * 4,
        out_specs=(anywhere, anywhere),
        scratch_shapes=[
            vector,
            pltpu.VMEM((points // 128, 128), jnp.int32),
            pltpu.VMEM((rank, points), F32),
            pltpu.VMEM((leaves, leaf, leaf), F32),
            pltpu.VMEM((leaves, leaf, leaf), BF16),
            pltpu.VMEM((leaves, leaf, leaf), BF16),
            pltpu.VMEM((rank, points), BF16),
            pltpu.VMEM((rank, points), BF16),
            pltpu.VMEM((points, rank), BF16),
            pltpu.VMEM((points, rank), BF16),
            pltpu.VMEM((16, rhs // 4, points), F32),
            pltpu.VMEM((2 * points, 128), F32),
            pltpu.VMEM((points, 128), F32),
            pltpu.VMEM((4, points // 128, 128), jnp.int32),
            pltpu.VMEM((4, points // 128, 128), jnp.int32),
            pltpu.SMEM((4, points // 128, 128), jnp.int32),
            pltpu.VMEM((4, rhs // 4, points), F32),
            pltpu.VMEM((2, rhs, points), F32), vector, vector, vector, vector,
            pltpu.VMEM((2, rhs, rank), F32),
            pltpu.VMEM((2, rhs, 4 * rhs), BF16),
            pltpu.VMEM((2, 16, 8, 128), F32),
            pltpu.VMEM((2, 16, 8, 128), F32),
            pltpu.VMEM((2, 16, 8, 128), F32),
            pltpu.VMEM((2, 8, 8, 128), F32),
            pltpu.VMEM((2, 16, 8, 128), F32),
            pltpu.VMEM((2, 16, rhs // 2 + 8, 2 * rhs), F32),
            pltpu.VMEM((2, 2, rhs // 2 + 8, 2 * rhs), F32),
            pltpu.VMEM((2, 4, rhs // 2 + 8, 2 * rhs), F32),
            dma((5,)), dma, dma((4,)), dma((4,)),
            dma((2, 4)), dma((2, 4)), dma((2, 4, 4)), dma((2, 4, 4)), dma((2, 4)), dma((2, 4)),
            dma((8, 4)), dma((8, 2, 4)), dma((16,)), dma((2, 16)),
            dma((3, 16)), dma((2, 3, 16)),
        ],
        compiler_params=pltpu.CompilerParams(
            collective_id=0, has_side_effects=True, vmem_limit_bytes=60 * 2**20
        ),
        name="block_cg",
    )(observations, order.reshape(points // 128, 128), leaf_blocks, factors.reshape(rank, points))


def solution(mesh):
    in_specs = (
        P(None, ("group", "sub")),
        P(("group", "sub")),
        P(("group", "sub"), None, None),
        P(None, None, ("group", "sub")),
    )
    out_specs = (P(None, ("group", "sub")), P(None, ("group", "sub")))
    return jax.shard_map(shards, mesh=mesh, in_specs=in_specs, out_specs=out_specs, check_vma=False)
```

```python
import functools

import jax
import jax.numpy as jnp
from jax import lax
from jax.experimental import pallas as pl
from jax.experimental.pallas import tpu as pltpu
from jax.sharding import PartitionSpec as P

ITERS = 4
FAR_FIRST = (10, 2, 8, 6, 14, 9, 11, 3, 7, 13, 15, 12, 5, 1, 4)
MESH = pl.DeviceIdType.MESH
F32 = jnp.float32
BF16 = jnp.bfloat16
EXACT = lax.Precision.HIGHEST
NT = (((1,), (1,)), ((), ()))


def halves(x):
    high = x.astype(BF16)
    return high, (x - high.astype(F32)).astype(BF16)


def dot3(left, right_high, right_low, dims=(((1,), (0,)), ((), ()))):
    rows = left.shape[0]
    high, low = halves(left)
    both = lax.dot_general(
        jnp.concatenate([high, low], 0), right_high, dims, preferred_element_type=F32
    )
    rest = lax.dot_general(high, right_low, dims, preferred_element_type=F32)
    return both[:rows] + (both[rows:] + rest)


def dot_exact(left, right, dims=(((1,), (0,)), ((), ()))):
    return lax.dot_general(left, right, dims, precision=EXACT, preferred_element_type=F32)


def eliminate(systems):
    size, lanes = systems[0].shape
    rows = lax.broadcasted_iota(jnp.int32, (8, lanes), 0)
    tiled = [[system[t : t + 8, :] for t in range(0, size, 8)] for system in systems]
    for k in range(0, size, 4):
        home, first = k // 8, k % 8
        done = []
        for tiles in tiled:
            columns = [
                [jnp.broadcast_to(tile[:, k + j : k + j + 1], (8, lanes)) for tile in tiles] for j in range(4)
            ]
            pivot = [[columns[j][home][first + i : first + i + 1, :] for j in range(4)] for i in range(4)]
            solved = [tiles[home][first + i : first + i + 1, :] for i in range(4)]
            for p in range(4):
                inverse = 1.0 / pivot[p][p]
                solved[p] = solved[p] * inverse
                scaled = [pivot[p][q] * inverse for q in range(p + 1, 4)]
                for i in range(4):
                    if i != p:
                        factor = pivot[i][p]
                        solved[i] = solved[i] - factor * solved[p]
                        for q in range(p + 1, 4):
                            pivot[i][q] = pivot[i][q] - factor * scaled[q - p - 1]
                for q in range(p + 1, 4):
                    pivot[p][q] = scaled[q - p - 1]
            fresh = []
            for t, tile in enumerate(tiles):
                tile = tile - (
                    (columns[0][t] * solved[0] + columns[1][t] * solved[1])
                    + (columns[2][t] * solved[2] + columns[3][t] * solved[3])
                )
                if t == home:
                    for i in range(4):
                        tile = jnp.where(rows == first + i, solved[i], tile)
                fresh.append(tile)
            done.append(fresh)
        tiled = done
    return [jnp.concatenate(tiles, 0) for tiles in tiled]


def total_of(pieces):
    while len(pieces) > 1:
        pieces = [pieces[i] + pieces[i + 1] for i in range(0, len(pieces), 2)]
    return pieces[0]


def fold(both):
    size = both.shape[0]
    row = lax.broadcasted_iota(jnp.int32, both.shape, 0)
    lane = lax.broadcasted_iota(jnp.int32, both.shape, 1)
    second = pltpu.roll(both, size, 1)
    merged = jnp.where(row >= lane, both, second)
    diagonal = jnp.sum(jnp.where(row == lane, second, 0.0), axis=0, keepdims=True)
    top, bottom = merged[: size // 2], pltpu.roll(merged[size // 2 :], size, 1)
    packed = jnp.where(lane[: size // 2] < size, top, bottom)
    return jnp.concatenate([packed, jnp.broadcast_to(diagonal, (8, 2 * size))], 0)


def unfold(packed):
    size = packed.shape[1] // 2
    top = packed[: size // 2]
    merged = jnp.concatenate([top, pltpu.roll(top, size, 1)], 0)[:, :size]
    turned = merged.T
    row = lax.broadcasted_iota(jnp.int32, merged.shape, 0)
    lane = lax.broadcasted_iota(jnp.int32, merged.shape, 1)
    diagonal = jnp.broadcast_to(packed[size // 2 : size // 2 + 1, :size], merged.shape)
    first = jnp.where(row >= lane, merged, turned)
    second = jnp.where(row == lane, diagonal, jnp.where(row < lane, merged, turned))
    return first, second


def kernel(
    obs_far, order_far, leaf_ref, factors_far,
    solution_ref, residual_ref,
    obs_ref, order_ref, factors_ref, stage, leaf_high, leaf_low, basis_high, basis_low, across_high, across_low,
    gathered, table, picked, order_in, source_in, order_smem, ready,
    r_ref, w_ref, d_ref, s_ref, x_ref, coef_ref, factor_ref,
    c_own, c_in, c_out, c_group, c_all, p_sum, c_sum, y_sum,
    load_sem, smem_sem, order_send, order_recv, near_send, near_recv, far_send, far_recv, back_send, back_recv,
    ring_send, ring_recv, plane_send, plane_recv, coef_send, coef_recv,
):
    group, sub = lax.axis_index("group"), lax.axis_index("sub")
    x = lax.rem(sub, 4)
    z = lax.div(sub, 4)
    core = lax.rem(group, 2)
    y = lax.div(group, 2)
    rhs, points = obs_ref.shape
    rank = factors_ref.shape[0]

    obs_load = pltpu.make_async_copy(obs_far, obs_ref, load_sem.at[2])
    order_load = pltpu.make_async_copy(order_far, order_ref, load_sem.at[3])
    factors_load = pltpu.make_async_copy(factors_far, factors_ref, load_sem.at[4])
    loads = [
        pltpu.make_async_copy(leaf_ref.at[b], stage.at[b], load_sem.at[b]) for b in range(2)
    ]
    for load in [order_load, obs_load, *loads, factors_load]:
        load.start()

    def on_x(k):
        return (group, z * 4 + (x ^ k))

    def on_z(k):
        return (group, (z ^ k) * 4 + x)

    def on_group(k):
        return (group ^ k, sub)

    def on_plane(k):
        return (group, sub ^ k)

    def on_core(k):
        return (y * 2 + (core ^ k), sub)

    def on_y(k):
        return ((y ^ k) * 2 + core, sub)

    def on_diagonal(j):
        return (group, lax.rem(z + j, 4) * 4 + lax.rem(x + j, 4))

    barrier = pltpu.get_barrier_semaphore()
    for peer in [on_plane(k) for k in range(1, 16)] + [on_group(k) for k in range(1, 8)]:
        pl.semaphore_signal(barrier, inc=1, device_id=peer, device_id_type=MESH)
    order_load.wait()
    obs_load.wait()
    pl.semaphore_wait(barrier, 22)

    def remote(source, target, sent, received, peer):
        copy = pltpu.make_async_remote_copy(
            src_ref=source, dst_ref=target, send_sem=sent, recv_sem=received,
            device_id=peer, device_id_type=MESH,
        )
        copy.start()
        return copy

    width = rhs // 8
    by_x, by_z = slice(0, width), slice(width, 2 * width)

    def x_rows(at):
        return pl.ds(pl.multiple_of(at * width, width), width)

    def z_rows(at):
        return pl.ds(pl.multiple_of(rhs // 2 + at * width, width), width)

    order_copies = [
        remote(order_ref, order_in.at[4 - j], order_send.at[j], order_recv.at[4 - j], on_diagonal(j))
        for j in range(1, 4)
    ]
    near = []
    for k in range(1, 4):
        near.append((
            remote(obs_ref.at[x_rows(x ^ k), :], gathered.at[sub, by_x], near_send.at[0, k], near_recv.at[0, k], on_x(k)),
            remote(obs_ref.at[z_rows(z ^ k), :], gathered.at[sub, by_z], near_send.at[1, k], near_recv.at[1, k], on_z(k)),
        ))
    far = []
    for m in range(1, 4):
        far.append(remote(obs_ref.at[x_rows(x), :], gathered.at[sub, by_x], far_send.at[0, 0, m], far_recv.at[0, 0, m], on_z(m)))
        far.append(remote(obs_ref.at[z_rows(z), :], gathered.at[sub, by_z], far_send.at[1, 0, m], far_recv.at[1, 0, m], on_x(m)))
    gathered[sub, by_x, :] = obs_ref[x_rows(x), :]
    gathered[sub, by_z, :] = obs_ref[z_rows(z), :]

    def cut_leaf(b):
        loads[b].wait()

        def cut(i, _):
            rows = pl.ds(pl.multiple_of(i * 64, 64), 64)
            leaf_high[b, rows, :], leaf_low[b, rows, :] = halves(stage[b, rows, :])
            return 0

        lax.fori_loop(0, leaf_ref.shape[1] // 64, cut, 0)

    cut_leaf(0)
    for k in range(1, 4):
        from_x, from_z = near[k - 1]
        from_x.wait()
        slot = gathered.at[z * 4 + (x ^ k), by_x]
        for m in range(1, 4):
            far.append(remote(slot, slot, far_send.at[0, k, m], far_recv.at[0, k, m], on_z(m)))
        from_z.wait()
        slot = gathered.at[(z ^ k) * 4 + x, by_z]
        for m in range(1, 4):
            far.append(remote(slot, slot, far_send.at[1, k, m], far_recv.at[1, k, m], on_x(m)))

    order_in[0] = order_ref[...]
    for copy in order_copies:
        copy.wait()
    for j in range(4):
        position = order_in[j]
        source_in[j] = lax.rem(lax.div(position, points), 8)
        order_in[j] = lax.div(position, points * 8) * points + lax.rem(position, points)
    to_scalar = pltpu.make_async_copy(order_in, order_smem, smem_sem)
    to_scalar.start()
    cut_leaf(1)

    def turn(i, _):
        cols = pl.ds(pl.multiple_of(i * 128, 128), 128)
        part = factors_ref[:, cols]
        basis_high[:, cols], basis_low[:, cols] = halves(part)
        across_high[cols, :], across_low[cols, :] = halves(part.T)
        return 0

    factors_load.wait()
    lax.fori_loop(0, points // 128, turn, 0)
    to_scalar.wait()
    for copy in far:
        copy.wait()

    def tabulate(i, _):
        for j in range(4):
            cols = pl.ds(pl.multiple_of(i * 512 + j * 128, 128), 128)
            for h in range(2):
                rows = pl.ds(pl.multiple_of(h * points + i * 512 + j * 128, 128), 128)
                table[rows, :] = gathered[8 * h : 8 * h + 8, :, cols].reshape(128, 128).T
        return 0

    lax.fori_loop(0, points // 512, tabulate, 0)

    back_copies = []
    for j in (2, 1, 3, 0):

        def pick(i, _, j=j):
            for n in range(128):
                picked[pl.ds(i * 128 + n, 1), :] = table[pl.ds(order_smem[j, i, n], 1), :]
            return 0

        lax.fori_loop(0, points // 128, pick, 0)

        def lay(i, _, j=j):
            for n in range(4):
                cols = pl.ds(pl.multiple_of(i * 512 + n * 128, 128), 128)
                turned = picked[cols, :].T
                source = source_in[j, pl.ds(i * 4 + n, 1), :]
                chosen = jnp.where(source == 0, turned[0 : 2 * width], 0.0)
                for g in range(1, 8):
                    chosen = jnp.where(source == g, turned[2 * width * g : 2 * width * (g + 1)], chosen)
                if j:
                    ready[j, :, cols] = chosen
                else:
                    r_ref[0, x_rows(x), cols] = chosen[by_x]
                    r_ref[0, z_rows(z), cols] = chosen[by_z]
            return 0

        lax.fori_loop(0, points // 512, lay, 0)
        if j:
            peer = on_diagonal(j)
            back_copies.append(remote(ready.at[j, by_x], r_ref.at[0, x_rows(x), :], back_send.at[0, j], back_recv.at[0, j], peer))
            back_copies.append(remote(ready.at[j, by_z], r_ref.at[0, z_rows(z), :], back_send.at[1, j], back_recv.at[1, j], peer))
    for copy in back_copies:
        copy.wait()

    def send(kind, turn_at, buffer, slot, peer, count):
        copies = []
        for k in range(1, count):
            copy = pltpu.make_async_remote_copy(
                src_ref=buffer.at[turn_at, slot], dst_ref=buffer.at[turn_at, slot],
                send_sem=ring_send.at[kind, k], recv_sem=ring_recv.at[kind, turn_at, k],
                device_id=peer(k), device_id_type=MESH,
            )
            copy.start()
            copies.append(copy)
        return copies

    def finish(copies):
        for copy in copies:
            copy.wait()

    d_ref[...] = jnp.zeros_like(d_ref)
    s_ref[...] = jnp.zeros_like(s_ref)
    x_ref[...] = jnp.zeros_like(x_ref)
    half = points // 2
    eye = (lax.broadcasted_iota(jnp.int32, (rhs, rhs), 0) == lax.broadcasted_iota(jnp.int32, (rhs, rhs), 1)).astype(F32)

    piece_lane = lax.broadcasted_iota(jnp.int32, (8, 128), 1)

    def by_level(parts):
        return jnp.where(
            piece_lane < 64,
            jnp.where(piece_lane < 32, parts[0], parts[1]),
            jnp.where(piece_lane < 96, parts[2], parts[3]),
        )

    def coef_scatter(at, own):
        for j in range(16):
            c_own[at, j] = own[8 * (j % 8) : 8 * (j % 8) + 8, 128 * (j // 8) : 128 * (j // 8) + 128]
        copies = [
            remote(c_own.at[at, sub ^ k], c_in.at[at, sub], coef_send.at[0, k], coef_recv.at[at, 0, k], on_plane(k))
            for k in FAR_FIRST
        ]
        c_in[at, sub] = c_own[at, sub]
        return copies

    def coef_groups(at, copies):
        finish(copies)
        sums = [[c_in[at, m] for m in range(16)]]
        for _ in range(4):
            sums.append([sums[-1][i] + sums[-1][i + 1] for i in range(0, len(sums[-1]), 2)])
        for m in range(16):
            c_out[at, m] = by_level([sums[level][m >> level] for level in range(4)])
        c_group[at, group] = sums[4][0]
        return [
            remote(c_group.at[at, group], c_group.at[at, group], coef_send.at[1, k], coef_recv.at[at, 1, k], on_group(k))
            for k in (6, 7, 4, 5, 2, 3, 1)
        ]

    def coef_return(at, copies):
        finish(copies)
        own = [c_group[at, group ^ k] for k in range(8)]
        pair = own[0] + own[1]
        four = pair + (own[2] + own[3])
        upper = by_level([own[0], pair, four, four + ((own[4] + own[5]) + (own[6] + own[7]))])
        for m in range(16):
            c_out[at, m] = jnp.where(sub < 8, c_out[at, m], upper)
        copies = [
            remote(c_out.at[at, sub ^ k], c_all.at[at, sub], coef_send.at[2, k], coef_recv.at[at, 2, k], on_plane(k))
            for k in FAR_FIRST
        ]
        c_all[at, sub] = c_out[at, sub]
        return copies

    def coef_whole(at, copies):
        finish(copies)
        return jnp.concatenate(
            [jnp.concatenate([c_all[at, j], c_all[at, j + 8]], 1) for j in range(8)], 0
        )

    def leaf_product(now):
        for b in range(2):
            cols = slice(b * half, (b + 1) * half)
            w_ref[:, cols] = dot3(r_ref[now, :, cols], leaf_high[b], leaf_low[b])

    def weights(matrix):
        high, low = halves(matrix)
        high, low = high.astype(F32), low.astype(F32)
        return jnp.concatenate([high, high, low, low], 0).T.astype(BF16)

    def times(weight, array):
        high, low = halves(array)
        return jnp.dot(
            weight, jnp.concatenate([high, low, high, low], 0), preferred_element_type=F32
        )

    def by_columns(step):
        def body(c, _):
            step(pl.ds(pl.multiple_of(c * 1024, 1024), 1024))
            return 0

        lax.fori_loop(0, points // 1024, body, 0)

    def advance_solution(before):
        def step(cols):
            fresh = r_ref[before, :, cols] + times(factor_ref[0], d_ref[:, cols])
            d_ref[:, cols] = fresh
            x_ref[:, cols] = x_ref[:, cols] + times(factor_ref[1], fresh)

        by_columns(step)

    copies = coef_scatter(1, dot3(r_ref[0], across_high[...], across_low[...]))
    leaf_product(0)
    coef_ref[0] = coef_whole(1, coef_return(1, coef_groups(1, copies)))
    coef_ref[1] = jnp.zeros((rhs, rank), F32)
    factor_ref[...] = jnp.zeros_like(factor_ref)

    def iteration(step, carry, more):
        inverse, curv_before = carry
        at = lax.rem(step, 2)
        now, later = at, 1 - at

        for c in range(4):
            cols = slice(c * 512, (c + 1) * 512)
            w_ref[:, cols] = w_ref[:, cols] + dot3(coef_ref[0], basis_high[:, cols], basis_low[:, cols])
        rw_high, rw_low = halves(jnp.concatenate([r_ref[now], w_ref[...]], 0))
        p_sum[at, sub] = fold(dot3(r_ref[now], rw_high, rw_low, NT))
        sums = [
            remote(p_sum.at[at, sub], p_sum.at[at, sub], plane_send.at[k], plane_recv.at[at, k], on_plane(k))
            for k in FAR_FIRST
        ]
        if more:
            copies = coef_scatter(at, dot3(w_ref[...], across_high[...], across_low[...]))

        finish(sums)
        c_sum[at, core] = total_of([p_sum[at, m] for m in range(16)])
        sums = send(5, at, c_sum, core, on_core, 2)
        if more:
            copies = coef_groups(at, copies)

        finish(sums)
        y_sum[at, y] = c_sum[at, 0] + c_sum[at, 1]
        sums = send(7, at, y_sum, y, on_y, 4)

        @pl.when(step > 0)
        def _():
            advance_solution(later)

        if more:
            copies = coef_return(at, copies)
        curv_inverse = dot_exact(curv_before, inverse)
        finish(sums)
        norm, along = unfold(total_of([y_sum[at, m] for m in range(4)]))
        beta = dot_exact(inverse, norm)
        beta_weight = weights(beta)
        factor_ref[0] = beta_weight
        curv = along - dot_exact(beta.T, dot_exact(curv_inverse, norm))

        def advance(cols):
            s_ref[:, cols] = w_ref[:, cols] + times(beta_weight, s_ref[:, cols])

        by_columns(advance)
        systems = [jnp.concatenate([curv, norm], 1)]
        if more:
            systems.append(jnp.concatenate([norm, eye], 1))
        done = eliminate(systems)
        alpha = done[0][:, rhs:]
        alpha_weight = weights(alpha)
        factor_ref[1] = alpha_weight

        def improve(cols):
            r_ref[later, :, cols] = r_ref[now, :, cols] - times(alpha_weight, s_ref[:, cols])

        by_columns(improve)
        if more:
            coef_ref[1] = coef_whole(at, copies) + dot_exact(beta.T, coef_ref[1])
            coef_ref[0] = coef_ref[0] - dot_exact(alpha.T, coef_ref[1])
            leaf_product(later)
        return done[-1][:, rhs:], curv

    zeros = jnp.zeros((rhs, rhs), F32)
    carry = lax.fori_loop(0, ITERS - 1, functools.partial(iteration, more=True), (zeros, zeros))
    iteration(ITERS - 1, carry, False)
    residual_out = pltpu.make_async_copy(r_ref.at[ITERS % 2], residual_ref, load_sem.at[0])
    residual_out.start()
    advance_solution((ITERS - 1) % 2)
    solution_out = pltpu.make_async_copy(x_ref, solution_ref, load_sem.at[1])
    solution_out.start()
    residual_out.wait()
    solution_out.wait()


def shards(observations, order, leaf_blocks, factors):
    rhs, points = observations.shape
    leaves, leaf = leaf_blocks.shape[:2]
    rank = factors.shape[0] * factors.shape[1]
    vector = pltpu.VMEM((rhs, points), F32)
    dma = pltpu.SemaphoreType.DMA
    anywhere = pl.BlockSpec(memory_space=pl.ANY)
    out = jax.ShapeDtypeStruct((rhs, points), F32)
    return pl.pallas_call(
        kernel,
        out_shape=(out, out),
        in_specs=[anywhere] * 4,
        out_specs=(anywhere, anywhere),
        scratch_shapes=[
            vector,
            pltpu.VMEM((points // 128, 128), jnp.int32),
            pltpu.VMEM((rank, points), F32),
            pltpu.VMEM((leaves, leaf, leaf), F32),
            pltpu.VMEM((leaves, leaf, leaf), BF16),
            pltpu.VMEM((leaves, leaf, leaf), BF16),
            pltpu.VMEM((rank, points), BF16),
            pltpu.VMEM((rank, points), BF16),
            pltpu.VMEM((points, rank), BF16),
            pltpu.VMEM((points, rank), BF16),
            pltpu.VMEM((16, rhs // 4, points), F32),
            pltpu.VMEM((2 * points, 128), F32),
            pltpu.VMEM((points, 128), F32),
            pltpu.VMEM((4, points // 128, 128), jnp.int32),
            pltpu.VMEM((4, points // 128, 128), jnp.int32),
            pltpu.SMEM((4, points // 128, 128), jnp.int32),
            pltpu.VMEM((4, rhs // 4, points), F32),
            pltpu.VMEM((2, rhs, points), F32), vector, vector, vector, vector,
            pltpu.VMEM((2, rhs, rank), F32),
            pltpu.VMEM((2, rhs, 4 * rhs), BF16),
            pltpu.VMEM((2, 16, 8, 128), F32),
            pltpu.VMEM((2, 16, 8, 128), F32),
            pltpu.VMEM((2, 16, 8, 128), F32),
            pltpu.VMEM((2, 8, 8, 128), F32),
            pltpu.VMEM((2, 16, 8, 128), F32),
            pltpu.VMEM((2, 16, rhs // 2 + 8, 2 * rhs), F32),
            pltpu.VMEM((2, 2, rhs // 2 + 8, 2 * rhs), F32),
            pltpu.VMEM((2, 4, rhs // 2 + 8, 2 * rhs), F32),
            dma((5,)), dma, dma((4,)), dma((4,)),
            dma((2, 4)), dma((2, 4)), dma((2, 4, 4)), dma((2, 4, 4)), dma((2, 4)), dma((2, 4)),
            dma((8, 4)), dma((8, 2, 4)), dma((16,)), dma((2, 16)),
            dma((3, 16)), dma((2, 3, 16)),
        ],
        compiler_params=pltpu.CompilerParams(
            collective_id=0, has_side_effects=True, vmem_limit_bytes=60 * 2**20
        ),
        name="block_cg",
    )(observations, order.reshape(points // 128, 128), leaf_blocks, factors.reshape(rank, points))


def solution(mesh):
    in_specs = (
        P(None, ("group", "sub")),
        P(("group", "sub")),
        P(("group", "sub"), None, None),
        P(None, None, ("group", "sub")),
    )
    out_specs = (P(None, ("group", "sub")), P(None, ("group", "sub")))
    return jax.shard_map(shards, mesh=mesh, in_specs=in_specs, out_specs=out_specs, check_vma=False)
```
